32 devices in a mesh: energy: 8 (over y, x, core), slab: 4 (over z).
Axes of the slice: x: 2, y: 2, z: 4, core: 2. Of those that a mesh axis runs over, the one named last changes fastest.
Arguments:
- slab_counts: int32 [4], replicated, may hold values from 2 to 4, as said below
- energy_index: int32 [8], replicated, may hold values from 0 to 31, as said below
- hamiltonian_blocks: float32 [16, 128, 128], P('slab'), as said below
- couplings: float32 [16, 128, 128], P('slab'), as said below
- injection: float32 [8, 16, 128, 128], P('energy', 'slab'), may hold values from -6 to 6
Outputs:
- lesser: float32 [8, 16, 128, 128], P('energy', 'slab')
- self_energy: float32 [8, 16, 128, 128], P(None, 'slab', 'energy')
The draws below stay inside these ranges and needn't reach their ends.
Inputs may be any that keep to these rules, and one draw needn't show every extreme that they name: `slab_counts`: each index holds 2 or more slabs, and some index holds exactly 4. `energy_index`: distinct and ascending; the first is 0 and the last 31. `hamiltonian_blocks`: symmetric; with the couplings, every operator M_e of the window is positive definite. `couplings`: with the Hamiltonian blocks, every operator M_e of the window is positive definite.
All inputs are finite; a program needn't handle non-finite values.
Results may differ from the reference program's by a relative error of at most 0.0003.
Values sent between devices are 32-bit elements; how exact they have to be, the bound alone decides.
A program may use at most 64 MiB of HBM per device.

```python
import math
import jax
import jax.numpy as jnp
from jax import lax

SLAB_ORBITALS = 128
LESSER_COLUMNS = 128
SLOT_CAPACITY = 4
NE = 8
NS = 16
GRID = 32
N_SLAB = 4


coupling_scale = 20.0


def draw_slab_counts(key, part):
    count_key, chosen_key = jax.random.split(key)
    counts = jax.random.randint(count_key, (N_SLAB,), 2, SLOT_CAPACITY + 1)
    chosen = jax.random.randint(chosen_key, (), 0, N_SLAB)
    return jnp.where(jnp.arange(N_SLAB) == chosen, SLOT_CAPACITY, counts).astype(jnp.int32)


def draw_energy_index(key, part):
    middle = jax.random.permutation(key, GRID - 2)[:NE - 2] + 1
    points = jnp.concatenate([jnp.zeros((1,), jnp.int32), middle.astype(jnp.int32), jnp.full((1,), GRID - 1, jnp.int32)])
    return jnp.sort(points).astype(jnp.int32)


def pair_partner(pair_key):
    ordering = jax.random.permutation(pair_key, SLAB_ORBITALS).astype(jnp.int32)
    firsts = ordering[0::2]
    seconds = ordering[1::2]
    numbers = jnp.arange(SLAB_ORBITALS // 2, dtype=jnp.int32)
    partner = jnp.zeros((SLAB_ORBITALS,), jnp.int32).at[firsts].set(seconds).at[seconds].set(firsts)
    leading = jnp.zeros((SLAB_ORBITALS,), jnp.int32).at[firsts].set(1)
    pair_id = jnp.zeros((SLAB_ORBITALS,), jnp.int32).at[firsts].set(numbers).at[seconds].set(numbers)
    return (partner, leading, pair_id)


def rotation_block(block_key):
    keys = jax.random.split(block_key, 5)
    row_order = jax.random.permutation(keys[0], SLAB_ORBITALS).astype(jnp.int32)
    col_order = jax.random.permutation(keys[1], SLAB_ORBITALS).astype(jnp.int32)
    row_signs = (2 * jax.random.randint(keys[2], (SLAB_ORBITALS,), 0, 2) - 1).astype(jnp.float32)
    frequency = row_order[:, None]
    phase = (2 * col_order[None, :] + 1) * frequency % (4 * SLAB_ORBITALS)
    cosine_base = math.sqrt(2.0 / SLAB_ORBITALS) * jnp.cos(math.pi * phase.astype(jnp.float32) / (2.0 * SLAB_ORBITALS))
    cosine_base = jnp.where(frequency == 0, cosine_base * math.sqrt(0.5), cosine_base)
    cosine_base = cosine_base * row_signs[:, None]
    partner, leading, pair_id = pair_partner(keys[3])
    angles = jax.random.uniform(keys[4], (SLAB_ORBITALS // 2,), jnp.float32, 0.3, 1.2)[pair_id]
    direction = jnp.where(leading == 1, -1.0, 1.0).astype(jnp.float32)
    return jnp.cos(angles)[:, None] * cosine_base + (direction * jnp.sin(angles))[:, None] * cosine_base[partner]


def onsite_block(block_key, low_pair, high_pair, low_margin, high_margin):
    keys = jax.random.split(block_key, 4)
    partner, leading, pair_id = pair_partner(keys[0])
    strength = jax.random.uniform(keys[1], (SLAB_ORBITALS // 2,), jnp.float32, low_pair, high_pair)[pair_id]
    pair_signs = (2 * jax.random.randint(keys[2], (SLAB_ORBITALS // 2,), 0, 2) - 1).astype(jnp.float32)[pair_id]
    margin = jnp.exp(jax.random.uniform(keys[3], (SLAB_ORBITALS,), jnp.float32, math.log(low_margin), math.log(high_margin)))
    columns = jnp.arange(SLAB_ORBITALS, dtype=jnp.int32)
    linked_slabs = (columns[None, :] == partner[:, None]).astype(jnp.float32)
    identity_matrix = jnp.eye(SLAB_ORBITALS, dtype=jnp.float32)
    return (2.0 * coupling_scale + strength + margin)[:, None] * identity_matrix - (pair_signs * strength)[:, None] * linked_slabs


def draw_hamiltonian_blocks(key, part):
    keys = jax.random.split(jax.random.fold_in(key, 11), NS)
    blocks = jax.vmap(lambda one_key: onsite_block(one_key, 0.005, 0.03, 0.001, 0.02))(keys)
    return blocks.astype(jnp.float32)


def draw_couplings(key, part):
    keys = jax.random.split(jax.random.fold_in(key, 23), NS)
    blocks = jax.vmap(rotation_block)(keys)
    return (-coupling_scale * blocks).astype(jnp.float32)


def shard_levels(stream_key, shape, cuts, smallest, top_value):
    gain = 1.0
    for position, shards_of in cuts:
        steps = jax.random.uniform(jax.random.fold_in(jax.random.fold_in(stream_key, 6), position), (shards_of,), jnp.float32, smallest / len(cuts), top_value / len(cuts))
        gain = gain * jnp.repeat(jnp.exp(steps), shape[position] // shards_of).reshape((-1,) + (1,) * (len(shape) - 1 - position))
    return gain


def centred(stream_key, extent, scale, limit, cuts=(), kind=jnp.bfloat16):
    values = jax.random.normal(stream_key, extent, jnp.float32) * scale
    if len(cuts) > 0:
        values = shard_levels(stream_key, extent, cuts, -0.22, 0.18) * values
    return jnp.clip(values, min=-limit, max=limit).astype(kind)


def setup_inputs(seed: int = 0) -> dict:
    seeds = jax.random.split(jax.random.key(seed), 6)
    slab_counts = draw_slab_counts(jax.random.fold_in(seeds[5], 71), 0)
    energy_index = draw_energy_index(jax.random.fold_in(seeds[5], 71), 0)
    hamiltonian_blocks = draw_hamiltonian_blocks(jax.random.fold_in(seeds[5], 71), 0)
    couplings = draw_couplings(jax.random.fold_in(seeds[5], 71), 0)
    injection = centred(seeds[4], (NE, NS, SLAB_ORBITALS, LESSER_COLUMNS), 1.0, 6.0, ((0, 8), (1, 4)), jnp.float32)
    return {"slab_counts": slab_counts, "energy_index": energy_index, "hamiltonian_blocks": hamiltonian_blocks, "couplings": couplings, "injection": injection}


precise_mode = lax.Precision.HIGHEST

def matmul(left, right):
    return jnp.dot(left.astype(jnp.float32), right.astype(jnp.float32), precision=precise_mode, preferred_element_type=jnp.float32)

def spd_solve(matrix, right):
    factor = jnp.linalg.cholesky(matrix)
    return jax.scipy.linalg.cho_solve((factor, True), right)

def kernel_table(energy_index):
    points = energy_index.astype(jnp.float32)
    offset = points[None, :] - points[:, None]
    return 0.5 * (1.6 * jnp.exp(-(offset - 6.0) ** 2 / 18.0) + 0.6 * jnp.exp(-(offset + 6.0) ** 2 / 18.0))

def reference(slab_counts, energy_index, hamiltonian_blocks, couplings, injection):
    slot_count = N_SLAB * SLOT_CAPACITY
    offsets = jnp.cumsum(slab_counts) - slab_counts
    total_sum = jnp.sum(slab_counts)
    slots = jnp.arange(SLOT_CAPACITY, dtype=jnp.int32)
    filled_slots = (slots[None, :] < slab_counts[:, None]).reshape(-1)
    slab_position = (offsets[:, None] + slots[None, :]).reshape(-1).astype(jnp.int32)
    target_block = jnp.where(filled_slots, slab_position, slot_count).astype(jnp.int32)
    identity_matrix = jnp.eye(SLAB_ORBITALS, dtype=jnp.float32)
    hamiltonian_matrix = jnp.broadcast_to(identity_matrix, (slot_count, SLAB_ORBITALS, SLAB_ORBITALS)).at[target_block].set(hamiltonian_blocks, mode='drop')
    linked_slabs = jnp.zeros((slot_count, SLAB_ORBITALS, SLAB_ORBITALS), jnp.float32).at[target_block].set(couplings, mode='drop')
    linked_slabs = linked_slabs * (jnp.arange(slot_count) < total_sum - 1).astype(jnp.float32)[:, None, None]
    shifts = 0.02 + 0.06 * energy_index.astype(jnp.float32) / GRID

    def solve_one(operands):
        shift_value, source_blocks = operands
        placed_blocks = jnp.zeros((slot_count, SLAB_ORBITALS, LESSER_COLUMNS), jnp.float32).at[target_block].set(source_blocks, mode='drop')
        diagonal = hamiltonian_matrix + shift_value * identity_matrix

        def forward(carry, item):
            prev_link, prev_w, prev_z = carry
            block, link, source = item
            schur = block - matmul(prev_link.T, prev_w)
            reduced = source - matmul(prev_link.T, prev_z)
            solved = spd_solve(schur, jnp.concatenate([link, reduced], axis=1))
            w_now = solved[:, :SLAB_ORBITALS]
            z_now = solved[:, SLAB_ORBITALS:]
            return ((link, w_now, z_now), (w_now, z_now))
        start = (jnp.zeros((SLAB_ORBITALS, SLAB_ORBITALS), jnp.float32), jnp.zeros((SLAB_ORBITALS, SLAB_ORBITALS), jnp.float32), jnp.zeros((SLAB_ORBITALS, LESSER_COLUMNS), jnp.float32))
        unused, (w_all, z_all) = lax.scan(forward, start, (diagonal, linked_slabs, placed_blocks))

        def backward(following, item):
            w_now, z_now = item
            value = z_now - matmul(w_now, following)
            return (value, value)
        unused_last, solution_block = lax.scan(backward, jnp.zeros((SLAB_ORBITALS, LESSER_COLUMNS), jnp.float32), (w_all, z_all), reverse=True)
        picked_rows = solution_block[jnp.minimum(slab_position, slot_count - 1)]
        return picked_rows * filled_slots.astype(jnp.float32)[:, None, None]
    lesser = lax.map(solve_one, (shifts, injection))
    table = kernel_table(energy_index)
    self_energy = jnp.einsum('ef,fsbk->esbk', table, lesser, precision=precise_mode)
    return (lesser, self_energy)
```

```python
import functools
import jax
import jax.numpy as jnp
from jax import lax
from jax.experimental import pallas as pl
from jax.experimental.pallas import tpu as pltpu
from jax.sharding import PartitionSpec as P

HIGHEST = lax.Precision.HIGHEST
MESH = pl.DeviceIdType.MESH


def contract(left, right, a, b):
    return lax.dot_general(
        left, right, (((a,), (b,)), ((), ())), precision=HIGHEST, preferred_element_type=jnp.float32
    )


def nn(left, right):
    return contract(left, right, 1, 0)


def tn(left, right):
    return contract(left, right, 0, 0)


def nt(left, right):
    return contract(left, right, 1, 1)


def spread(x, q):
    return jnp.broadcast_to(x[q : q + 1, :], (8, 128))


def across(x, k):
    return jnp.take_along_axis(x, jnp.full((8, 128), k, jnp.int32), axis=1)


def tree(terms):
    while len(terms) > 1:
        terms = [terms[i] + terms[i + 1] for i in range(0, len(terms), 2)]
    return terms[0]


def pivot_rows(rows, columns, sub):
    for q in range(0, 8, 2):
        first, both = sub == q, (sub == q) | (sub == q + 1)
        x, y = columns[q], columns[q + 1]
        a, b, d = spread(x, q), spread(y, q), spread(y, q + 1)
        inv = 1.0 / (a * d - b * b)
        gx = jnp.where(both, jnp.where(first, -1.0, 0.0), x)
        gy = jnp.where(both, jnp.where(first, 0.0, -1.0), y)
        fx = d * gx - b * gy
        fy = a * gy - b * gx
        ex, ey = fx * inv, fy * inv
        for j in range(q + 2, 8):
            u, v = spread(columns[j], q), spread(columns[j], q + 1)
            rest = jnp.where(both, 0.0, columns[j])
            change = (fx * u + fy * v) * inv if j < q + 4 else ex * u + ey * v
            columns[j] = rest - change
        change = ex * spread(rows, q) + ey * spread(rows, q + 1)
        rows = jnp.where(both, 0.0, rows) - change
    return rows


def sweep(chunks, at, k, lane, sub):
    columns = [[across(c, k + q) for c in chunks] for q in range(8)]
    inside = (lane >= k) & (lane < k + 8)
    pivots = jnp.where(inside, jnp.where(lane - k == sub, -1.0, 0.0), chunks[at])
    solved = pivot_rows(pivots, [column[at] for column in columns], sub)
    rows = [spread(solved, q) for q in range(8)]
    out = []
    for c in range(len(chunks)):
        if c == at:
            out.append(solved)
        else:
            change = tree([columns[q][c] * rows[q] for q in range(8)])
            out.append(jnp.where(inside, 0.0, chunks[c]) - change)
    return out


def inverses(matrices):
    width = matrices[0].shape[0]
    size = width // 2 if len(matrices) == 1 else width // 4
    lane = lax.broadcasted_iota(jnp.int32, (8, 128), 1)
    sub = lax.broadcasted_iota(jnp.int32, (8, 128), 0)
    count = width // 8
    sets = [[m[8 * i : 8 * i + 8, :] for i in range(count)] for m in matrices]
    for start in range(0, width, size):
        low, high = start // 8, (start + size) // 8
        panels = [s[low:high] for s in sets]
        for g in range(high - low):
            panels = [sweep(p, g, start + 8 * g, lane, sub) for p in panels]
        for i in range(len(sets)):
            rest = jnp.concatenate(sets[i][:low] + sets[i][high:], axis=0)
            zero = jnp.zeros((8, width), jnp.float32)
            panel = jnp.concatenate([zero] * low + panels[i] + [zero] * (count - high), axis=0)
            column = lax.broadcasted_iota(jnp.int32, rest.shape, 1)
            inside = (column >= start) & (column < start + size)
            rest = jnp.where(inside, 0.0, rest) - nn(rest, panel)
            rest = [rest[8 * j : 8 * j + 8, :] for j in range(count - high + low)]
            sets[i] = rest[:low] + panels[i] + rest[low:]
    return [-jnp.concatenate(s, axis=0) for s in sets]


def kernel(
    ne, nslab, counts_in, energies_in, ham_in, link_in, inj_in, lesser, selfe,
    counts, energies, ham, link, inj, si,
    keep, out_a, in_a, out_b, in_b, out_c, in_c, out_d, in_d, out_e, in_e, weights,
    sa, ra, sb, rb, sc, rc, sd, rd, se, re,
):
    pairs = [
        (counts_in, counts), (energies_in, energies), (ham_in, ham), (link_in, link), (inj_in, inj)
    ]
    staged = [pltpu.make_async_copy(a, b, si.at[i]) for i, (a, b) in enumerate(pairs)]
    for copy in staged:
        copy.start()
    e = lax.axis_index("energy")
    p = lax.axis_index("slab")
    half = nslab // 2
    width = ham.shape[1]
    cap = ham.shape[0]
    rows = width // ne
    is_left = p < half
    is_outer = (p == 0) | (p == nslab - 1)
    is_middle = (p == half - 1) | (p == half)
    takes_a = (p > 0) & (p <= half)
    inward = jnp.where(is_left, p + 1, p - 1)
    outward = jnp.where(is_left, p - 1, p + 1)

    barrier = pltpu.get_barrier_semaphore()
    for i in range(1, ne):
        pl.semaphore_signal(
            barrier, inc=1, device_id=(lax.rem(e + i, ne), p), device_id_type=MESH
        )

    @pl.when(p > 0)
    def _():
        pl.semaphore_signal(barrier, inc=1, device_id=(e, p - 1), device_id_type=MESH)

    @pl.when(p < nslab - 1)
    def _():
        pl.semaphore_signal(barrier, inc=1, device_id=(e, p + 1), device_id_type=MESH)

    def send(src, dst, send_sem, recv_sem, to):
        return pltpu.make_async_remote_copy(
            src_ref=src, dst_ref=dst, send_sem=send_sem, recv_sem=recv_sem,
            device_id=(e, to), device_id_type=MESH,
        )

    for copy in staged:
        copy.wait()
    shape = (width, width)
    eye = (
        lax.broadcasted_iota(jnp.int32, shape, 0) == lax.broadcasted_iota(jnp.int32, shape, 1)
    ).astype(jnp.float32)
    shift = 0.02 + 0.06 * energies[e].astype(jnp.float32) / (4 * ne)
    shifted = eye * shift
    count = jnp.full(shape, counts[p], jnp.int32)
    two, three, four = count == 2, count >= 3, count == 4
    inner = jnp.full(shape, p, jnp.int32) < nslab - 1
    zero = jnp.zeros(shape, jnp.float32)

    diag_a = jnp.where(three, ham[1] + shifted, eye)
    diag_d = jnp.where(four, ham[3] + shifted, eye)
    inv_a, inv_d = inverses([diag_a, diag_d])
    link_0a = jnp.where(three, link[0], zero)
    link_0b = jnp.where(three, zero, link[0])
    link_ab = jnp.where(three, link[1], zero)
    link_bd = jnp.where(four, link[2], zero)
    link_dt = jnp.where(four & inner, link[3], zero)
    link_bt = jnp.where(inner, jnp.where(two, link[1], jnp.where(four, zero, link[2])), zero)
    rhs_a = jnp.where(three, inj[0, 1], zero)
    rhs_b = jnp.where(three, inj[0, 2], inj[0, 1])
    rhs_d = jnp.where(four, inj[0, 3], zero)
    diag_b = jnp.where(three, ham[2], ham[1]) + shifted

    xab = nn(inv_a, link_ab)
    xdb = nt(inv_d, link_bd)
    diag_b = diag_b - tn(link_ab, xab) - nn(link_bd, xdb)
    keep[2] = inv_a
    keep[3] = inv_d
    keep[4] = xab
    keep[6] = xdb
    (inv_b,) = inverses([diag_b])

    def send_a(i):
        return send(out_a.at[i], in_a.at[i], sa.at[i], ra.at[i], p + 1)

    def send_b(i):
        return send(out_b.at[i], in_b.at[i], sb.at[i], rb.at[i], inward)

    def send_c(i):
        return send(out_c.at[i], in_c.at[i], sc.at[i], rc.at[i], inward)

    def send_d():
        return send(out_d, in_d, sd, rd, outward)

    inv_a, inv_d, xab, xdb = keep[2], keep[3], keep[4], keep[6]
    link_0b = link_0b - nn(link_0a, xab)
    xa0 = nt(inv_a, link_0a)
    xb0 = nt(inv_b, link_0b)
    node = ham[0] + shifted - nn(link_0a, xa0) - nn(link_0b, xb0)
    keep[0] = node
    out_b[0] = node
    keep[2] = xa0
    keep[8] = xb0

    pl.semaphore_wait(barrier, ne - 1 + jnp.where(is_outer, 1, 2))

    @pl.when(p == nslab - 1)
    def _():
        send_b(0).start()

    xdt = nn(inv_d, link_dt)
    link_bt = link_bt - nn(link_bd, xdt)
    xbt = nn(inv_b, link_bt)
    out_a[0] = tn(link_dt, xdt) + tn(link_bt, xbt)
    keep[5] = xdt
    keep[9] = xbt

    @pl.when(is_left)
    def _():
        send_a(0).start()

    xaf = nn(inv_a, rhs_a)
    xdf = nn(inv_d, rhs_d)
    rhs_b = rhs_b - tn(link_ab, xaf) - nn(link_bd, xdf)
    xbf = nn(inv_b, rhs_b)
    node_rhs = inj[0, 0] - nn(link_0a, xaf) - nn(link_0b, xbf)
    keep[1] = node_rhs
    out_b[1] = node_rhs

    @pl.when(p == nslab - 1)
    def _():
        send_b(1).start()

    out_a[1] = tn(link_dt, xdf) + tn(link_bt, xbf)
    out_a[2] = -tn(link_bt, xb0)

    @pl.when(is_left)
    def _():
        send_a(1).start()

    @pl.when(p == half - 1)
    def _():
        send_a(2).start()

    own_link = -nn(link_0b, xbt)
    keep[3], keep[7], keep[10] = xaf, xdf, xbf
    keep[11] = own_link
    keep[12] = own_link

    @pl.when(jnp.logical_not(is_left) & jnp.logical_not(is_outer))
    def _():
        send_b(0).wait_recv()
        (inv_t,) = inverses([in_b[0] - out_a[0]])
        xj = nt(inv_t, keep[11])
        keep[0] = keep[0] - nn(keep[11], xj)
        send_b(1).wait_recv()
        xr = nn(inv_t, in_b[1] - out_a[1])
        keep[1] = keep[1] - nn(keep[11], xr)
        keep[13] = xj
        keep[14] = xr

        @pl.when(jnp.logical_not(is_middle))
        def _():
            out_b[0] = keep[0]
            send_b(0).start()
            out_b[1] = keep[1]
            send_b(1).start()

    @pl.when(takes_a)
    def _():
        send_a(0).wait_recv()
        send_a(1).wait_recv()
        keep[0] = keep[0] - in_a[0]
        keep[1] = keep[1] - in_a[1]

    @pl.when(is_left & jnp.logical_not(is_outer))
    def _():
        send_b(0).wait_recv()
        keep[0] = keep[0] - in_b[0]

    @pl.when(is_left | is_middle)
    def _():
        (inv_n,) = inverses([keep[0]])
        keep[15] = inv_n

    @pl.when(is_left & jnp.logical_not(is_outer))
    def _():
        send_b(1).wait_recv()
        keep[1] = keep[1] - in_b[1]

    @pl.when(is_middle & jnp.logical_not(is_left))
    def _():
        send_a(2).wait_recv()
        keep[12] = in_a[2]

    @pl.when(is_middle)
    def _():
        inv_n = keep[15]
        out_c[0] = nn(inv_n, keep[12])
        send_c(0).start()
        out_c[1] = nn(inv_n, keep[1])
        send_c(1).start()
        send_c(0).wait_recv()
        (inv_m,) = inverses([keep[0] - nn(keep[12], in_c[0])])
        send_c(1).wait_recv()
        x0 = nn(inv_m, keep[1] - nn(keep[12], in_c[1]))
        out_d[...] = x0

        @pl.when(is_left & jnp.logical_not(is_outer))
        def _():
            send_d().start()

        in_d[...] = in_c[1] - nn(in_c[0], x0)
        send_c(0).wait_send()
        send_c(1).wait_send()

    @pl.when(is_left & jnp.logical_not(is_middle))
    def _():
        inv_n = keep[15]
        xj = nn(inv_n, keep[12])
        out_b[0] = tn(keep[12], xj)
        send_b(0).start()
        xr = nn(inv_n, keep[1])
        out_b[1] = tn(keep[12], xr)
        send_b(1).start()
        send_d().wait_recv()
        out_d[...] = xr - nn(xj, in_d[...])

    @pl.when(is_left & jnp.logical_not(is_outer) & jnp.logical_not(is_middle))
    def _():
        send_d().start()

    @pl.when(is_left)
    def _():
        keep[0] = in_d[...]
        keep[1] = out_d[...]

    @pl.when(jnp.logical_not(is_left))
    def _():
        @pl.when(is_middle)
        def _():
            keep[1] = out_d[...]

        @pl.when(jnp.logical_not(is_middle))
        def _():
            send_d().wait_recv()
            keep[1] = in_d[...]

        @pl.when(is_outer)
        def _():
            keep[0] = jnp.zeros(shape, jnp.float32)

        @pl.when(jnp.logical_not(is_outer))
        def _():
            following = keep[14] - nn(keep[13], keep[1])
            keep[0] = following
            out_d[...] = following
            send_d().start()

    @pl.when(jnp.logical_not(is_middle))
    def _():
        send_b(0).wait_send()
        send_b(1).wait_send()

    x0, xt = keep[1], keep[0]
    xb = keep[10] - nn(keep[8], x0) - nn(keep[9], xt)
    xa = keep[3] - nn(keep[2], x0) - nn(keep[4], xb)
    xd = keep[7] - nn(keep[5], xt) - nn(keep[6], xb)
    blocks = [
        x0, jnp.where(three, xa, xb), jnp.where(three, xb, zero), jnp.where(four, xd, zero)
    ]
    for j in range(cap):
        for i in range(ne):
            out_e[i, j * rows : (j + 1) * rows, :] = blocks[j][i * rows : (i + 1) * rows, :]

    def send_e(i):
        to = lax.rem(e + i, ne)
        return pltpu.make_async_remote_copy(
            src_ref=out_e.at[to], dst_ref=in_e.at[e], send_sem=se.at[i], recv_sem=re.at[i],
            device_id=(to, p), device_id_type=MESH,
        )

    for i in range(1, ne):
        send_e(i).start()
    for j in range(cap):
        lesser[0, j] = blocks[j]
    in_e[e] = out_e[e]

    def weights_of(k, carry):
        here = energies[k].astype(jnp.float32)
        for f in range(ne):
            t = jnp.full((8, 128), energies[f].astype(jnp.float32) - here, jnp.float32)
            weights[k, f] = 0.5 * (
                1.6 * jnp.exp(-((t - 6.0) ** 2) / 18.0) + 0.6 * jnp.exp(-((t + 6.0) ** 2) / 18.0)
            )
        return carry

    lax.fori_loop(0, ne, weights_of, 0)
    for i in range(1, ne):
        send_e(i).wait_recv()

    def row_of(k, carry):
        terms = [weights[k, f][:1] * in_e[f] for f in range(ne)]
        while len(terms) > 1:
            pairs = [terms[i : i + 2] for i in range(0, len(terms), 2)]
            terms = [q[0] + q[1] if len(q) == 2 else q[0] for q in pairs]
        for j in range(cap):
            selfe[k, j] = terms[0][j * rows : (j + 1) * rows, :]
        return carry

    lax.fori_loop(0, ne, row_of, 0)
    for i in range(1, ne):
        send_e(i).wait_send()

    @pl.when(is_left)
    def _():
        send_a(0).wait_send()
        send_a(1).wait_send()

    @pl.when(p == half - 1)
    def _():
        send_a(2).wait_send()

    @pl.when(jnp.logical_not(is_outer))
    def _():
        send_d().wait_send()


def per_device(ne, nslab, counts, energies, ham, link, inj):
    cap, width, _ = ham.shape
    rows = width // ne
    block = lambda *n: pltpu.VMEM((*n, width, width), jnp.float32)
    dma = pltpu.SemaphoreType.DMA
    vmem = pl.BlockSpec(memory_space=pltpu.VMEM)
    hbm = pl.BlockSpec(memory_space=pltpu.HBM)
    exchange = pltpu.VMEM((ne, cap * rows, width), jnp.float32)
    return pl.pallas_call(
        functools.partial(kernel, ne, nslab),
        out_shape=(
            jax.ShapeDtypeStruct(inj.shape, jnp.float32),
            jax.ShapeDtypeStruct((ne, cap, rows, width), jnp.float32),
        ),
        in_specs=[hbm] * 5,
        out_specs=(vmem, vmem),
        scratch_shapes=[
            pltpu.SMEM(counts.shape, jnp.int32), pltpu.SMEM(energies.shape, jnp.int32),
            pltpu.VMEM(ham.shape, jnp.float32), pltpu.VMEM(link.shape, jnp.float32),
            pltpu.VMEM(inj.shape, jnp.float32), dma((5,)),
            block(16), block(3), block(3), block(2), block(2), block(2), block(2), block(), block(),
            exchange, exchange, pltpu.VMEM((ne, ne, 8, 128), jnp.float32),
            dma((3,)), dma((3,)), dma((2,)), dma((2,)), dma((2,)), dma((2,)), dma, dma,
            dma((ne,)), dma((ne,)),
        ],
        compiler_params=pltpu.CompilerParams(
            collective_id=0, has_side_effects=True, vmem_limit_bytes=62 << 20
        ),
    )(counts, energies, ham, link, inj)


def solution(mesh):
    return jax.shard_map(
        functools.partial(per_device, mesh.shape["energy"], mesh.shape["slab"]),
        mesh=mesh,
        in_specs=(
            P(),
            P(),
            P("slab", None, None),
            P("slab", None, None),
            P("energy", "slab", None, None),
        ),
        out_specs=(P("energy", "slab", None, None), P(None, "slab", "energy", None)),
        check_vma=False,
    )
```

```python
import functools
import jax
import jax.numpy as jnp
from jax import lax
from jax.experimental import pallas as pl
from jax.experimental.pallas import tpu as pltpu
from jax.sharding import PartitionSpec as P

HIGHEST = lax.Precision.HIGHEST
MESH = pl.DeviceIdType.MESH


def contract(left, right, a, b):
    return lax.dot_general(
        left, right, (((a,), (b,)), ((), ())), precision=HIGHEST, preferred_element_type=jnp.float32
    )


def nn(left, right):
    return contract(left, right, 1, 0)


def tn(left, right):
    return contract(left, right, 0, 0)


def nt(left, right):
    return contract(left, right, 1, 1)


def spread(x, q):
    return jnp.broadcast_to(x[q : q + 1, :], (8, 128))


def across(x, k):
    return jnp.take_along_axis(x, jnp.full((8, 128), k, jnp.int32), axis=1)


def tree(terms):
    while len(terms) > 1:
        terms = [terms[i] + terms[i + 1] for i in range(0, len(terms), 2)]
    return terms[0]


def pivot_rows(rows, columns, sub):
    for q in range(0, 8, 2):
        first, both = sub == q, (sub == q) | (sub == q + 1)
        x, y = columns[q], columns[q + 1]
        a, b, d = spread(x, q), spread(y, q), spread(y, q + 1)
        inv = 1.0 / (a * d - b * b)
        gx = jnp.where(both, jnp.where(first, -1.0, 0.0), x)
        gy = jnp.where(both, jnp.where(first, 0.0, -1.0), y)
        fx = d * gx - b * gy
        fy = a * gy - b * gx
        ex, ey = fx * inv, fy * inv
        for j in range(q + 2, 8):
            u, v = spread(columns[j], q), spread(columns[j], q + 1)
            rest = jnp.where(both, 0.0, columns[j])
            change = (fx * u + fy * v) * inv if j < q + 4 else ex * u + ey * v
            columns[j] = rest - change
        change = ex * spread(rows, q) + ey * spread(rows, q + 1)
        rows = jnp.where(both, 0.0, rows) - change
    return rows


def sweep(chunks, at, k, lane, sub):
    columns = [[across(c, k + q) for c in chunks] for q in range(8)]
    inside = (lane >= k) & (lane < k + 8)
    pivots = jnp.where(inside, jnp.where(lane - k == sub, -1.0, 0.0), chunks[at])
    solved = pivot_rows(pivots, [column[at] for column in columns], sub)
    rows = [spread(solved, q) for q in range(8)]
    out = []
    for c in range(len(chunks)):
        if c == at:
            out.append(solved)
        else:
            change = tree([columns[q][c] * rows[q] for q in range(8)])
            out.append(jnp.where(inside, 0.0, chunks[c]) - change)
    return out


def inverses(matrices):
    width = matrices[0].shape[0]
    size = width // 2 if len(matrices) == 1 else width // 4
    lane = lax.broadcasted_iota(jnp.int32, (8, 128), 1)
    sub = lax.broadcasted_iota(jnp.int32, (8, 128), 0)
    count = width // 8
    sets = [[m[8 * i : 8 * i + 8, :] for i in range(count)] for m in matrices]
    for start in range(0, width, size):
        low, high = start // 8, (start + size) // 8
        panels = [s[low:high] for s in sets]
        for g in range(high - low):
            panels = [sweep(p, g, start + 8 * g, lane, sub) for p in panels]
        for i in range(len(sets)):
            rest = jnp.concatenate(sets[i][:low] + sets[i][high:], axis=0)
            zero = jnp.zeros((8, width), jnp.float32)
            panel = jnp.concatenate([zero] * low + panels[i] + [zero] * (count - high), axis=0)
            column = lax.broadcasted_iota(jnp.int32, rest.shape, 1)
            inside = (column >= start) & (column < start + size)
            rest = jnp.where(inside, 0.0, rest) - nn(rest, panel)
            rest = [rest[8 * j : 8 * j + 8, :] for j in range(count - high + low)]
            sets[i] = rest[:low] + panels[i] + rest[low:]
    return [-jnp.concatenate(s, axis=0) for s in sets]


def kernel(
    ne, nslab, counts_in, energies_in, ham_in, link_in, inj_in, lesser, selfe,
    counts, energies, ham, link, inj, si,
    keep, out_a, in_a, out_b, in_b, out_c, in_c, out_d, in_d, out_e, in_e, weights,
    sa, ra, sb, rb, sc, rc, sd, rd, se, re,
):
    pairs = [
        (counts_in, counts), (energies_in, energies), (ham_in, ham), (link_in, link), (inj_in, inj)
    ]
    staged = [pltpu.make_async_copy(a, b, si.at[i]) for i, (a, b) in enumerate(pairs)]
    for copy in staged:
        copy.start()
    e = lax.axis_index("energy")
    p = lax.axis_index("slab")
    half = nslab // 2
    width = ham.shape[1]
    cap = ham.shape[0]
    rows = width // ne
    is_left = p < half
    is_outer = (p == 0) | (p == nslab - 1)
    is_middle = (p == half - 1) | (p == half)
    takes_a = (p > 0) & (p <= half)
    inward = jnp.where(is_left, p + 1, p - 1)
    outward = jnp.where(is_left, p - 1, p + 1)

    barrier = pltpu.get_barrier_semaphore()
    for i in range(1, ne):
        pl.semaphore_signal(
            barrier, inc=1, device_id=(lax.rem(e + i, ne), p), device_id_type=MESH
        )

    @pl.when(p > 0)
    def _():
        pl.semaphore_signal(barrier, inc=1, device_id=(e, p - 1), device_id_type=MESH)

    @pl.when(p < nslab - 1)
    def _():
        pl.semaphore_signal(barrier, inc=1, device_id=(e, p + 1), device_id_type=MESH)

    def send(src, dst, send_sem, recv_sem, to):
        return pltpu.make_async_remote_copy(
            src_ref=src, dst_ref=dst, send_sem=send_sem, recv_sem=recv_sem,
            device_id=(e, to), device_id_type=MESH,
        )

    for copy in staged:
        copy.wait()
    shape = (width, width)
    eye = (
        lax.broadcasted_iota(jnp.int32, shape, 0) == lax.broadcasted_iota(jnp.int32, shape, 1)
    ).astype(jnp.float32)
    shift = 0.02 + 0.06 * energies[e].astype(jnp.float32) / (4 * ne)
    shifted = eye * shift
    count = jnp.full(shape, counts[p], jnp.int32)
    two, three, four = count == 2, count >= 3, count == 4
    inner = jnp.full(shape, p, jnp.int32) < nslab - 1
    zero = jnp.zeros(shape, jnp.float32)

    diag_a = jnp.where(three, ham[1] + shifted, eye)
    diag_d = jnp.where(four, ham[3] + shifted, eye)
    inv_a, inv_d = inverses([diag_a, diag_d])
    link_0a = jnp.where(three, link[0], zero)
    link_0b = jnp.where(three, zero, link[0])
    link_ab = jnp.where(three, link[1], zero)
    link_bd = jnp.where(four, link[2], zero)
    link_dt = jnp.where(four & inner, link[3], zero)
    link_bt = jnp.where(inner, jnp.where(two, link[1], jnp.where(four, zero, link[2])), zero)
    rhs_a = jnp.where(three, inj[0, 1], zero)
    rhs_b = jnp.where(three, inj[0, 2], inj[0, 1])
    rhs_d = jnp.where(four, inj[0, 3], zero)
    diag_b = jnp.where(three, ham[2], ham[1]) + shifted

    xab = nn(inv_a, link_ab)
    xdb = nt(inv_d, link_bd)
    diag_b = diag_b - tn(link_ab, xab) - nn(link_bd, xdb)
    keep[2] = inv_a
    keep[3] = inv_d
    keep[4] = xab
    keep[6] = xdb
    (inv_b,) = inverses([diag_b])

    def send_a(i):
        return send(out_a.at[i], in_a.at[i], sa.at[i], ra.at[i], p + 1)

    def send_b(i):
        return send(out_b.at[i], in_b.at[i], sb.at[i], rb.at[i], inward)

    def send_c(i):
        return send(out_c.at[i], in_c.at[i], sc.at[i], rc.at[i], inward)

    def send_d():
        return send(out_d, in_d, sd, rd, outward)

    inv_a, inv_d, xab, xdb = keep[2], keep[3], keep[4], keep[6]
    link_0b = link_0b - nn(link_0a, xab)
    xa0 = nt(inv_a, link_0a)
    xb0 = nt(inv_b, link_0b)
    node = ham[0] + shifted - nn(link_0a, xa0) - nn(link_0b, xb0)
    keep[0] = node
    out_b[0] = node
    keep[2] = xa0
    keep[8] = xb0

    pl.semaphore_wait(barrier, ne - 1 + jnp.where(is_outer, 1, 2))

    @pl.when(p == nslab - 1)
    def _():
        send_b(0).start()

    xdt = nn(inv_d, link_dt)
    link_bt = link_bt - nn(link_bd, xdt)
    xbt = nn(inv_b, link_bt)
    out_a[0] = tn(link_dt, xdt) + tn(link_bt, xbt)
    keep[5] = xdt
    keep[9] = xbt

    @pl.when(is_left)
    def _():
        send_a(0).start()

    xaf = nn(inv_a, rhs_a)
    xdf = nn(inv_d, rhs_d)
    rhs_b = rhs_b - tn(link_ab, xaf) - nn(link_bd, xdf)
    xbf = nn(inv_b, rhs_b)
    node_rhs = inj[0, 0] - nn(link_0a, xaf) - nn(link_0b, xbf)
    keep[1] = node_rhs
    out_b[1] = node_rhs

    @pl.when(p == nslab - 1)
    def _():
        send_b(1).start()

    out_a[1] = tn(link_dt, xdf) + tn(link_bt, xbf)
    out_a[2] = -tn(link_bt, xb0)

    @pl.when(is_left)
    def _():
        send_a(1).start()

    @pl.when(p == half - 1)
    def _():
        send_a(2).start()

    own_link = -nn(link_0b, xbt)
    keep[3], keep[7], keep[10] = xaf, xdf, xbf
    keep[11] = own_link
    keep[12] = own_link

    @pl.when(jnp.logical_not(is_left) & jnp.logical_not(is_outer))
    def _():
        send_b(0).wait_recv()
        (inv_t,) = inverses([in_b[0] - out_a[0]])
        xj = nt(inv_t, keep[11])
        keep[0] = keep[0] - nn(keep[11], xj)
        send_b(1).wait_recv()
        xr = nn(inv_t, in_b[1] - out_a[1])
        keep[1] = keep[1] - nn(keep[11], xr)
        keep[13] = xj
        keep[14] = xr

        @pl.when(jnp.logical_not(is_middle))
        def _():
            out_b[0] = keep[0]
            send_b(0).start()
            out_b[1] = keep[1]
            send_b(1).start()

    @pl.when(takes_a)
    def _():
        send_a(0).wait_recv()
        send_a(1).wait_recv()
        keep[0] = keep[0] - in_a[0]
        keep[1] = keep[1] - in_a[1]

    @pl.when(is_left & jnp.logical_not(is_outer))
    def _():
        send_b(0).wait_recv()
        keep[0] = keep[0] - in_b[0]

    @pl.when(is_left | is_middle)
    def _():
        (inv_n,) = inverses([keep[0]])
        keep[15] = inv_n

    @pl.when(is_left & jnp.logical_not(is_outer))
    def _():
        send_b(1).wait_recv()
        keep[1] = keep[1] - in_b[1]

    @pl.when(is_middle & jnp.logical_not(is_left))
    def _():
        send_a(2).wait_recv()
        keep[12] = in_a[2]

    @pl.when(is_middle)
    def _():
        inv_n = keep[15]
        out_c[0] = nn(inv_n, keep[12])
        send_c(0).start()
        out_c[1] = nn(inv_n, keep[1])
        send_c(1).start()
        send_c(0).wait_recv()
        (inv_m,) = inverses([keep[0] - nn(keep[12], in_c[0])])
        send_c(1).wait_recv()
        x0 = nn(inv_m, keep[1] - nn(keep[12], in_c[1]))
        out_d[...] = x0

        @pl.when(is_left & jnp.logical_not(is_outer))
        def _():
            send_d().start()

        in_d[...] = in_c[1] - nn(in_c[0], x0)
        send_c(0).wait_send()
        send_c(1).wait_send()

    @pl.when(is_left & jnp.logical_not(is_middle))
    def _():
        inv_n = keep[15]
        xj = nn(inv_n, keep[12])
        out_b[0] = tn(keep[12], xj)
        send_b(0).start()
        xr = nn(inv_n, keep[1])
        out_b[1] = tn(keep[12], xr)
        send_b(1).start()
        send_d().wait_recv()
        out_d[...] = xr - nn(xj, in_d[...])

    @pl.when(is_left & jnp.logical_not(is_outer) & jnp.logical_not(is_middle))
    def _():
        send_d().start()

    @pl.when(is_left)
    def _():
        keep[0] = in_d[...]
        keep[1] = out_d[...]

    @pl.when(jnp.logical_not(is_left))
    def _():
        @pl.when(is_middle)
        def _():
            keep[1] = out_d[...]

        @pl.when(jnp.logical_not(is_middle))
        def _():
            send_d().wait_recv()
            keep[1] = in_d[...]

        @pl.when(is_outer)
        def _():
            keep[0] = jnp.zeros(shape, jnp.float32)

        @pl.when(jnp.logical_not(is_outer))
        def _():
            following = keep[14] - nn(keep[13], keep[1])
            keep[0] = following
            out_d[...] = following
            send_d().start()

    @pl.when(jnp.logical_not(is_middle))
    def _():
        send_b(0).wait_send()
        send_b(1).wait_send()

    x0, xt = keep[1], keep[0]
    xb = keep[10] - nn(keep[8], x0) - nn(keep[9], xt)
    xa = keep[3] - nn(keep[2], x0) - nn(keep[4], xb)
    xd = keep[7] - nn(keep[5], xt) - nn(keep[6], xb)
    blocks = [
        x0, jnp.where(three, xa, xb), jnp.where(three, xb, zero), jnp.where(four, xd, zero)
    ]
    for j in range(cap):
        for i in range(ne):
            out_e[i, j * rows : (j + 1) * rows, :] = blocks[j][i * rows : (i + 1) * rows, :]

    def send_e(i):
        to = lax.rem(e + i, ne)
        return pltpu.make_async_remote_copy(
            src_ref=out_e.at[to], dst_ref=in_e.at[e], send_sem=se.at[i], recv_sem=re.at[i],
            device_id=(to, p), device_id_type=MESH,
        )

    for i in range(1, ne):
        send_e(i).start()
    for j in range(cap):
        lesser[0, j] = blocks[j]
    in_e[e] = out_e[e]

    def weights_of(k, carry):
        here = energies[k].astype(jnp.float32)
        for f in range(ne):
            t = jnp.full((8, 128), energies[f].astype(jnp.float32) - here, jnp.float32)
            weights[k, f] = 0.5 * (
                1.6 * jnp.exp(-((t - 6.0) ** 2) / 18.0) + 0.6 * jnp.exp(-((t + 6.0) ** 2) / 18.0)
            )
        return carry

    lax.fori_loop(0, ne, weights_of, 0)
    for i in range(1, ne):
        send_e(i).wait_recv()

    def row_of(k, carry):
        terms = [weights[k, f][:1] * in_e[f] for f in range(ne)]
        while len(terms) > 1:
            pairs = [terms[i : i + 2] for i in range(0, len(terms), 2)]
            terms = [q[0] + q[1] if len(q) == 2 else q[0] for q in pairs]
        for j in range(cap):
            selfe[k, j] = terms[0][j * rows : (j + 1) * rows, :]
        return carry

    lax.fori_loop(0, ne, row_of, 0)
    for i in range(1, ne):
        send_e(i).wait_send()

    @pl.when(is_left)
    def _():
        send_a(0).wait_send()
        send_a(1).wait_send()

    @pl.when(p == half - 1)
    def _():
        send_a(2).wait_send()

    @pl.when(jnp.logical_not(is_outer))
    def _():
        send_d().wait_send()


def short_kernel(
    ne, nslab, counts_in, energies_in, ham_in, link_in, inj_in, lesser, selfe,
    counts, energies, ham, link, inj, si,
    keep, here, there, out_e, in_e, weights, ss, rs, se, re,
):
    pairs = [
        (counts_in, counts), (energies_in, energies), (ham_in, ham), (link_in, link), (inj_in, inj)
    ]
    staged = [pltpu.make_async_copy(a, b, si.at[i]) for i, (a, b) in enumerate(pairs)]
    for copy in staged:
        copy.start()
    e = lax.axis_index("energy")
    p = lax.axis_index("slab")
    width = ham.shape[1]
    cap = ham.shape[0]
    rows = width // ne
    last = nslab - 1
    is_outer = (p == 0) | (p == last)
    is_left = p < 2
    near = jnp.where(is_left, 1 - p, 5 - p)
    middle = jnp.where(is_left, 2, 1)
    far = last - p

    barrier = pltpu.get_barrier_semaphore()
    for i in range(1, ne):
        pl.semaphore_signal(
            barrier, inc=1, device_id=(lax.rem(e + i, ne), p), device_id_type=MESH
        )
    for i in range(1, nslab):
        pl.semaphore_signal(
            barrier, inc=1, device_id=(e, lax.rem(p + i, nslab)), device_id_type=MESH
        )

    C, N, K, R, A0, A1, S0, S1, X, Y, D0, D1 = range(12)

    def send(what, slot, to):
        return pltpu.make_async_remote_copy(
            src_ref=here.at[what], dst_ref=there.at[what],
            send_sem=ss.at[slot], recv_sem=rs.at[what],
            device_id=(e, to), device_id_type=MESH,
        )

    def arrived(what):
        send(what, what, near).wait_recv()

    def from_inner():
        return [send(N, N, near), send(K, K, near), send(R, R, near)]

    def from_second():
        return [send(A0, A0, 2), send(A1, A1, 2)]

    def from_third(i):
        return [send(S0 + i, 12 + 3 * i + j, to) for j, to in enumerate((0, 1, last))]

    def from_outer(i):
        return [
            send(D0 + i, 18 + 2 * i, far), send(D0 + i, 19 + 2 * i, middle), send(X + i, X + i, near)
        ]

    for copy in staged:
        copy.wait()
    shape = (width, width)
    eye = (
        lax.broadcasted_iota(jnp.int32, shape, 0) == lax.broadcasted_iota(jnp.int32, shape, 1)
    ).astype(jnp.float32)
    shift = 0.02 + 0.06 * energies[e].astype(jnp.float32) / (4 * ne)
    shifted = eye * shift
    at = jnp.full(shape, p, jnp.int32)
    third, inner = at == 2, at < last
    count = jnp.full(shape, counts[p], jnp.int32) - third.astype(jnp.int32)
    one, two, three, four = count == 1, count == 2, count >= 3, count == 4
    zero = jnp.zeros(shape, jnp.float32)

    def ending(blocks):
        return jnp.where(one, blocks[1], jnp.where(two, blocks[2], blocks[3]))

    here[C] = ending(link).T
    diag_a = jnp.where(three, ham[1] + shifted, eye)
    diag_d = jnp.where(four, ham[3] + shifted, eye)
    inv_a, inv_d = inverses([diag_a, diag_d])
    link_0a = jnp.where(three, link[0], zero)
    link_0b = jnp.where(two, link[0], zero)
    link_0t = jnp.where(one, link[0], zero)
    link_ab = jnp.where(three, link[1], zero)
    link_bd = jnp.where(four, link[2], zero)
    link_dt = jnp.where(four & inner, link[3], zero)
    link_bt = jnp.where(two & inner, link[1], jnp.where((count == 3) & inner, link[2], zero))
    rhs_a = jnp.where(three, inj[0, 1], zero)
    rhs_b = jnp.where(three, inj[0, 2], jnp.where(two, inj[0, 1], zero))
    rhs_d = jnp.where(four, inj[0, 3], zero)
    diag_b = jnp.where(three, ham[2] + shifted, jnp.where(two, ham[1] + shifted, eye))

    xab = nn(inv_a, link_ab)
    xdb = nt(inv_d, link_bd)
    diag_b = diag_b - tn(link_ab, xab) - nn(link_bd, xdb)
    keep[2] = inv_a
    keep[3] = inv_d
    keep[4] = xab
    keep[6] = xdb
    pl.semaphore_wait(barrier, ne + nslab - 2)

    @pl.when(p == 2)
    def _():
        send(C, C, last).start()

    inv_a, inv_d, xab, xdb = keep[2], keep[3], keep[4], keep[6]
    (inv_b,) = inverses([diag_b])
    link_0b = link_0b - nn(link_0a, xab)
    xa0 = nt(inv_a, link_0a)
    xdt = nn(inv_d, link_dt)
    link_bt = link_bt - nn(link_bd, xdt)
    xb0 = nt(inv_b, link_0b)
    xbt = nn(inv_b, link_bt)
    node = ham[0] + shifted - nn(link_0a, xa0) - nn(link_0b, xb0)
    ahead = tn(link_dt, xdt) + tn(link_bt, xbt)
    keep[0] = node
    here[A0] = ahead
    here[N] = jnp.where(third, ending(ham) + shifted - ahead, node)

    @pl.when(jnp.logical_not(is_outer))
    def _():
        from_inner()[0].start()

    @pl.when(p == 1)
    def _():
        from_second()[0].start()

    own_link = link_0t - nn(link_0b, xbt)
    here[K] = jnp.where(third, own_link.T, own_link)
    keep[2] = xa0
    keep[5] = xdt
    keep[8] = xb0
    keep[9] = xbt

    @pl.when(jnp.logical_not(is_outer))
    def _():
        from_inner()[1].start()

    xaf = nn(inv_a, rhs_a)
    xdf = nn(inv_d, rhs_d)
    rhs_b = rhs_b - tn(link_ab, xaf) - nn(link_bd, xdf)
    xbf = nn(inv_b, rhs_b)
    node_rhs = inj[0, 0] - nn(link_0a, xaf) - nn(link_0b, xbf)
    ahead = tn(link_dt, xdf) + tn(link_bt, xbf)
    keep[1] = node_rhs
    here[A1] = ahead
    here[R] = jnp.where(third, ending(inj.at[0]) - ahead, node_rhs)
    keep[3], keep[7], keep[10] = xaf, xdf, xbf

    @pl.when(jnp.logical_not(is_outer))
    def _():
        from_inner()[2].start()

    @pl.when(p == 1)
    def _():
        from_second()[1].start()

    @pl.when(p == 2)
    def _():
        arrived(A0)
        here[S0] = keep[0] - there[A0]
        for copy in from_third(0):
            copy.start()
        arrived(A1)
        here[S1] = keep[1] - there[A1]
        for copy in from_third(1):
            copy.start()

    @pl.when(is_outer)
    def _():
        (inv_n,) = inverses([keep[0]])
        keep[15] = inv_n

        @pl.when(p == 0)
        def _():
            keep[11] = here[K]

        @pl.when(p == last)
        def _():
            arrived(C)
            keep[11] = there[C]

        xj = nn(keep[15], keep[11])
        keep[12] = xj
        arrived(N)
        (inv_m,) = inverses([there[N] - here[A0] - tn(keep[11], xj)])
        keep[14] = inv_m
        xr = nn(keep[15], keep[1])
        keep[13] = xr
        below = here[A1] + tn(keep[11], xr)
        arrived(K)
        x = nn(inv_m, there[K])
        here[X] = x
        here[D0] = tn(there[K], x)
        for copy in from_outer(0):
            copy.start()
        arrived(R)
        y = nn(keep[14], there[R] - below)
        here[Y] = y
        here[D1] = tn(there[K], y)
        for copy in from_outer(1):
            copy.start()

    @pl.when(jnp.logical_not(is_outer))
    def _():
        arrived(X)
        x = there[X]
        here[X] = x
        here[D0] = tn(here[K], x)

    @pl.when(p != 2)
    def _():
        arrived(S0)
        here[S0] = there[S0]

    arrived(D0)
    (inv_s,) = inverses([here[S0] - here[D0] - there[D0]])
    keep[15] = inv_s

    @pl.when(jnp.logical_not(is_outer))
    def _():
        arrived(Y)
        y = there[Y]
        here[Y] = y
        here[D1] = tn(here[K], y)

    @pl.when(p != 2)
    def _():
        arrived(S1)
        here[S1] = there[S1]

    arrived(D1)
    x2 = nn(keep[15], here[S1] - here[D1] - there[D1])
    end = here[Y] - nn(here[X], x2)

    @pl.when(is_outer)
    def _():
        keep[0] = end
        keep[1] = keep[13] - nn(keep[12], end)

    @pl.when(jnp.logical_not(is_outer))
    def _():
        keep[0] = jnp.where(third, end, x2)
        keep[1] = jnp.where(third, x2, end)

    x0, xt = keep[1], keep[0]
    xb = keep[10] - nn(keep[8], x0) - nn(keep[9], xt)
    xa = keep[3] - nn(keep[2], x0) - nn(keep[4], xb)
    xd = keep[7] - nn(keep[5], xt) - nn(keep[6], xb)
    blocks = [
        x0,
        jnp.where(three, xa, jnp.where(one, xt, xb)),
        jnp.where(three, xb, jnp.where(two & third, xt, zero)),
        jnp.where(four, xd, jnp.where(three & third, xt, zero)),
    ]
    for j in range(cap):
        for i in range(ne):
            out_e[i, j * rows : (j + 1) * rows, :] = blocks[j][i * rows : (i + 1) * rows, :]

    def send_e(i):
        to = lax.rem(e + i, ne)
        return pltpu.make_async_remote_copy(
            src_ref=out_e.at[to], dst_ref=in_e.at[e], send_sem=se.at[i], recv_sem=re.at[i],
            device_id=(to, p), device_id_type=MESH,
        )

    for i in range(1, ne):
        send_e(i).start()
    for j in range(cap):
        lesser[0, j] = blocks[j]
    in_e[e] = out_e[e]

    def weights_of(k, carry):
        here = energies[k].astype(jnp.float32)
        for f in range(ne):
            t = jnp.full((8, 128), energies[f].astype(jnp.float32) - here, jnp.float32)
            weights[k, f] = 0.5 * (
                1.6 * jnp.exp(-((t - 6.0) ** 2) / 18.0) + 0.6 * jnp.exp(-((t + 6.0) ** 2) / 18.0)
            )
        return carry

    lax.fori_loop(0, ne, weights_of, 0)
    for i in range(1, ne):
        send_e(i).wait_recv()

    def row_of(k, carry):
        terms = [weights[k, f][:1] * in_e[f] for f in range(ne)]
        while len(terms) > 1:
            pairs = [terms[i : i + 2] for i in range(0, len(terms), 2)]
            terms = [q[0] + q[1] if len(q) == 2 else q[0] for q in pairs]
        for j in range(cap):
            selfe[k, j] = terms[0][j * rows : (j + 1) * rows, :]
        return carry

    lax.fori_loop(0, ne, row_of, 0)
    for i in range(1, ne):
        send_e(i).wait_send()

    @pl.when(jnp.logical_not(is_outer))
    def _():
        for copy in from_inner():
            copy.wait_send()

    @pl.when(is_outer)
    def _():
        for copy in from_outer(0) + from_outer(1):
            copy.wait_send()

    @pl.when(p == 1)
    def _():
        for copy in from_second():
            copy.wait_send()

    @pl.when(p == 2)
    def _():
        for copy in [send(C, C, last)] + from_third(0) + from_third(1):
            copy.wait_send()


def per_device(ne, nslab, counts, energies, ham, link, inj):
    cap, width, _ = ham.shape
    rows = width // ne
    block = lambda *n: pltpu.VMEM((*n, width, width), jnp.float32)
    dma = pltpu.SemaphoreType.DMA
    vmem = pl.BlockSpec(memory_space=pltpu.VMEM)
    hbm = pl.BlockSpec(memory_space=pltpu.HBM)
    exchange = pltpu.VMEM((ne, cap * rows, width), jnp.float32)
    staging = [
        pltpu.SMEM(counts.shape, jnp.int32), pltpu.SMEM(energies.shape, jnp.int32),
        pltpu.VMEM(ham.shape, jnp.float32), pltpu.VMEM(link.shape, jnp.float32),
        pltpu.VMEM(inj.shape, jnp.float32), dma((5,)),
    ]
    last = [exchange, exchange, pltpu.VMEM((ne, ne, 8, 128), jnp.float32)]
    if nslab == 4:
        body = short_kernel
        scratch = [block(16), block(12), block(12), *last, dma((22,)), dma((12,))]
    else:
        body = kernel
        scratch = [
            block(16), block(3), block(3), block(2), block(2), block(2), block(2), block(), block(),
            *last, dma((3,)), dma((3,)), dma((2,)), dma((2,)), dma((2,)), dma((2,)), dma, dma,
        ]
    return pl.pallas_call(
        functools.partial(body, ne, nslab),
        out_shape=(
            jax.ShapeDtypeStruct(inj.shape, jnp.float32),
            jax.ShapeDtypeStruct((ne, cap, rows, width), jnp.float32),
        ),
        in_specs=[hbm] * 5,
        out_specs=(vmem, vmem),
        scratch_shapes=[*staging, *scratch, dma((ne,)), dma((ne,))],
        compiler_params=pltpu.CompilerParams(
            collective_id=0, has_side_effects=True, vmem_limit_bytes=62 << 20
        ),
    )(counts, energies, ham, link, inj)


def solution(mesh):
    return jax.shard_map(
        functools.partial(per_device, mesh.shape["energy"], mesh.shape["slab"]),
        mesh=mesh,
        in_specs=(
            P(),
            P(),
            P("slab", None, None),
            P("slab", None, None),
            P("energy", "slab", None, None),
        ),
        out_specs=(P("energy", "slab", None, None), P(None, "slab", "energy", None)),
        check_vma=False,
    )
```

```python
import functools
import jax
import jax.numpy as jnp
from jax import lax
from jax.experimental import pallas as pl
from jax.experimental.pallas import tpu as pltpu
from jax.sharding import PartitionSpec as P

HIGHEST = lax.Precision.HIGHEST
MESH = pl.DeviceIdType.MESH


def contract(left, right, a, b):
    return lax.dot_general(
        left, right, (((a,), (b,)), ((), ())), precision=HIGHEST, preferred_element_type=jnp.float32
    )


def nn(left, right):
    return contract(left, right, 1, 0)


def tn(left, right):
    return contract(left, right, 0, 0)


def nt(left, right):
    return contract(left, right, 1, 1)


def spread(x, q):
    return jnp.broadcast_to(x[q : q + 1, :], (8, 128))


def across(x, k):
    return jnp.take_along_axis(x, jnp.full((8, 128), k, jnp.int32), axis=1)


def tree(terms):
    while len(terms) > 1:
        terms = [terms[i] + terms[i + 1] for i in range(0, len(terms), 2)]
    return terms[0]


def pivot_rows(rows, columns, sub):
    for q in range(0, 8, 2):
        first, both = sub == q, (sub == q) | (sub == q + 1)
        x, y = columns[q], columns[q + 1]
        a, b, d = spread(x, q), spread(y, q), spread(y, q + 1)
        inv = 1.0 / (a * d - b * b)
        gx = jnp.where(both, jnp.where(first, -1.0, 0.0), x)
        gy = jnp.where(both, jnp.where(first, 0.0, -1.0), y)
        fx = d * gx - b * gy
        fy = a * gy - b * gx
        ex, ey = fx * inv, fy * inv
        for j in range(q + 2, 8):
            u, v = spread(columns[j], q), spread(columns[j], q + 1)
            rest = jnp.where(both, 0.0, columns[j])
            change = (fx * u + fy * v) * inv if j < q + 4 else ex * u + ey * v
            columns[j] = rest - change
        change = ex * spread(rows, q) + ey * spread(rows, q + 1)
        rows = jnp.where(both, 0.0, rows) - change
    return rows


def sweep(chunks, at, k, lane, sub):
    columns = [[across(c, k + q) for c in chunks] for q in range(8)]
    inside = (lane >= k) & (lane < k + 8)
    pivots = jnp.where(inside, jnp.where(lane - k == sub, -1.0, 0.0), chunks[at])
    solved = pivot_rows(pivots, [column[at] for column in columns], sub)
    rows = [spread(solved, q) for q in range(8)]
    out = []
    for c in range(len(chunks)):
        if c == at:
            out.append(solved)
        else:
            change = tree([columns[q][c] * rows[q] for q in range(8)])
            out.append(jnp.where(inside, 0.0, chunks[c]) - change)
    return out


def inverses(matrices):
    width = matrices[0].shape[0]
    size = width // 2 if len(matrices) == 1 else width // 4
    lane = lax.broadcasted_iota(jnp.int32, (8, 128), 1)
    sub = lax.broadcasted_iota(jnp.int32, (8, 128), 0)
    count = width // 8
    sets = [[m[8 * i : 8 * i + 8, :] for i in range(count)] for m in matrices]
    for start in range(0, width, size):
        low, high = start // 8, (start + size) // 8
        panels = [s[low:high] for s in sets]
        for g in range(high - low):
            panels = [sweep(p, g, start + 8 * g, lane, sub) for p in panels]
        for i in range(len(sets)):
            rest = jnp.concatenate(sets[i][:low] + sets[i][high:], axis=0)
            zero = jnp.zeros((8, width), jnp.float32)
            panel = jnp.concatenate([zero] * low + panels[i] + [zero] * (count - high), axis=0)
            column = lax.broadcasted_iota(jnp.int32, rest.shape, 1)
            inside = (column >= start) & (column < start + size)
            rest = jnp.where(inside, 0.0, rest) - nn(rest, panel)
            rest = [rest[8 * j : 8 * j + 8, :] for j in range(count - high + low)]
            sets[i] = rest[:low] + panels[i] + rest[low:]
    return [-jnp.concatenate(s, axis=0) for s in sets]


def kernel(
    ne, nslab, counts_in, energies_in, ham_in, link_in, inj_in, lesser, selfe,
    counts, energies, ham, link, inj, si,
    keep, out_a, in_a, out_b, in_b, out_c, in_c, out_d, in_d, out_e, in_e, weights,
    sa, ra, sb, rb, sc, rc, sd, rd, se, re,
):
    pairs = [
        (counts_in, counts), (energies_in, energies), (ham_in, ham), (link_in, link), (inj_in, inj)
    ]
    staged = [pltpu.make_async_copy(a, b, si.at[i]) for i, (a, b) in enumerate(pairs)]
    for copy in staged:
        copy.start()
    e = lax.axis_index("energy")
    p = lax.axis_index("slab")
    half = nslab // 2
    width = ham.shape[1]
    cap = ham.shape[0]
    rows = width // ne
    is_left = p < half
    is_outer = (p == 0) | (p == nslab - 1)
    is_middle = (p == half - 1) | (p == half)
    takes_a = (p > 0) & (p <= half)
    inward = jnp.where(is_left, p + 1, p - 1)
    outward = jnp.where(is_left, p - 1, p + 1)

    barrier = pltpu.get_barrier_semaphore()
    for i in range(1, ne):
        pl.semaphore_signal(
            barrier, inc=1, device_id=(lax.rem(e + i, ne), p), device_id_type=MESH
        )

    @pl.when(p > 0)
    def _():
        pl.semaphore_signal(barrier, inc=1, device_id=(e, p - 1), device_id_type=MESH)

    @pl.when(p < nslab - 1)
    def _():
        pl.semaphore_signal(barrier, inc=1, device_id=(e, p + 1), device_id_type=MESH)

    def send(src, dst, send_sem, recv_sem, to):
        return pltpu.make_async_remote_copy(
            src_ref=src, dst_ref=dst, send_sem=send_sem, recv_sem=recv_sem,
            device_id=(e, to), device_id_type=MESH,
        )

    for copy in staged:
        copy.wait()
    shape = (width, width)
    eye = (
        lax.broadcasted_iota(jnp.int32, shape, 0) == lax.broadcasted_iota(jnp.int32, shape, 1)
    ).astype(jnp.float32)
    shift = 0.02 + 0.06 * energies[e].astype(jnp.float32) / (4 * ne)
    shifted = eye * shift
    count = jnp.full(shape, counts[p], jnp.int32)
    two, three, four = count == 2, count >= 3, count == 4
    inner = jnp.full(shape, p, jnp.int32) < nslab - 1
    zero = jnp.zeros(shape, jnp.float32)

    diag_a = jnp.where(three, ham[1] + shifted, eye)
    diag_d = jnp.where(four, ham[3] + shifted, eye)
    inv_a, inv_d = inverses([diag_a, diag_d])
    link_0a = jnp.where(three, link[0], zero)
    link_0b = jnp.where(three, zero, link[0])
    link_ab = jnp.where(three, link[1], zero)
    link_bd = jnp.where(four, link[2], zero)
    link_dt = jnp.where(four & inner, link[3], zero)
    link_bt = jnp.where(inner, jnp.where(two, link[1], jnp.where(four, zero, link[2])), zero)
    rhs_a = jnp.where(three, inj[0, 1], zero)
    rhs_b = jnp.where(three, inj[0, 2], inj[0, 1])
    rhs_d = jnp.where(four, inj[0, 3], zero)
    diag_b = jnp.where(three, ham[2], ham[1]) + shifted

    xab = nn(inv_a, link_ab)
    xdb = nt(inv_d, link_bd)
    diag_b = diag_b - tn(link_ab, xab) - nn(link_bd, xdb)
    keep[2] = inv_a
    keep[3] = inv_d
    keep[4] = xab
    keep[6] = xdb
    (inv_b,) = inverses([diag_b])

    def send_a(i):
        return send(out_a.at[i], in_a.at[i], sa.at[i], ra.at[i], p + 1)

    def send_b(i):
        return send(out_b.at[i], in_b.at[i], sb.at[i], rb.at[i], inward)

    def send_c(i):
        return send(out_c.at[i], in_c.at[i], sc.at[i], rc.at[i], inward)

    def send_d():
        return send(out_d, in_d, sd, rd, outward)

    inv_a, inv_d, xab, xdb = keep[2], keep[3], keep[4], keep[6]
    link_0b = link_0b - nn(link_0a, xab)
    xa0 = nt(inv_a, link_0a)
    xb0 = nt(inv_b, link_0b)
    node = ham[0] + shifted - nn(link_0a, xa0) - nn(link_0b, xb0)
    keep[0] = node
    out_b[0] = node
    keep[2] = xa0
    keep[8] = xb0

    pl.semaphore_wait(barrier, ne - 1 + jnp.where(is_outer, 1, 2))

    @pl.when(p == nslab - 1)
    def _():
        send_b(0).start()

    xdt = nn(inv_d, link_dt)
    link_bt = link_bt - nn(link_bd, xdt)
    xbt = nn(inv_b, link_bt)
    out_a[0] = tn(link_dt, xdt) + tn(link_bt, xbt)
    keep[5] = xdt
    keep[9] = xbt

    @pl.when(is_left)
    def _():
        send_a(0).start()

    xaf = nn(inv_a, rhs_a)
    xdf = nn(inv_d, rhs_d)
    rhs_b = rhs_b - tn(link_ab, xaf) - nn(link_bd, xdf)
    xbf = nn(inv_b, rhs_b)
    node_rhs = inj[0, 0] - nn(link_0a, xaf) - nn(link_0b, xbf)
    keep[1] = node_rhs
    out_b[1] = node_rhs

    @pl.when(p == nslab - 1)
    def _():
        send_b(1).start()

    out_a[1] = tn(link_dt, xdf) + tn(link_bt, xbf)
    out_a[2] = -tn(link_bt, xb0)

    @pl.when(is_left)
    def _():
        send_a(1).start()

    @pl.when(p == half - 1)
    def _():
        send_a(2).start()

    own_link = -nn(link_0b, xbt)
    keep[3], keep[7], keep[10] = xaf, xdf, xbf
    keep[11] = own_link
    keep[12] = own_link

    @pl.when(jnp.logical_not(is_left) & jnp.logical_not(is_outer))
    def _():
        send_b(0).wait_recv()
        (inv_t,) = inverses([in_b[0] - out_a[0]])
        xj = nt(inv_t, keep[11])
        keep[0] = keep[0] - nn(keep[11], xj)
        send_b(1).wait_recv()
        xr = nn(inv_t, in_b[1] - out_a[1])
        keep[1] = keep[1] - nn(keep[11], xr)
        keep[13] = xj
        keep[14] = xr

        @pl.when(jnp.logical_not(is_middle))
        def _():
            out_b[0] = keep[0]
            send_b(0).start()
            out_b[1] = keep[1]
            send_b(1).start()

    @pl.when(takes_a)
    def _():
        send_a(0).wait_recv()
        send_a(1).wait_recv()
        keep[0] = keep[0] - in_a[0]
        keep[1] = keep[1] - in_a[1]

    @pl.when(is_left & jnp.logical_not(is_outer))
    def _():
        send_b(0).wait_recv()
        keep[0] = keep[0] - in_b[0]

    @pl.when(is_left | is_middle)
    def _():
        (inv_n,) = inverses([keep[0]])
        keep[15] = inv_n

    @pl.when(is_left & jnp.logical_not(is_outer))
    def _():
        send_b(1).wait_recv()
        keep[1] = keep[1] - in_b[1]

    @pl.when(is_middle & jnp.logical_not(is_left))
    def _():
        send_a(2).wait_recv()
        keep[12] = in_a[2]

    @pl.when(is_middle)
    def _():
        inv_n = keep[15]
        out_c[0] = nn(inv_n, keep[12])
        send_c(0).start()
        out_c[1] = nn(inv_n, keep[1])
        send_c(1).start()
        send_c(0).wait_recv()
        (inv_m,) = inverses([keep[0] - nn(keep[12], in_c[0])])
        send_c(1).wait_recv()
        x0 = nn(inv_m, keep[1] - nn(keep[12], in_c[1]))
        out_d[...] = x0

        @pl.when(is_left & jnp.logical_not(is_outer))
        def _():
            send_d().start()

        in_d[...] = in_c[1] - nn(in_c[0], x0)
        send_c(0).wait_send()
        send_c(1).wait_send()

    @pl.when(is_left & jnp.logical_not(is_middle))
    def _():
        inv_n = keep[15]
        xj = nn(inv_n, keep[12])
        out_b[0] = tn(keep[12], xj)
        send_b(0).start()
        xr = nn(inv_n, keep[1])
        out_b[1] = tn(keep[12], xr)
        send_b(1).start()
        send_d().wait_recv()
        out_d[...] = xr - nn(xj, in_d[...])

    @pl.when(is_left & jnp.logical_not(is_outer) & jnp.logical_not(is_middle))
    def _():
        send_d().start()

    @pl.when(is_left)
    def _():
        keep[0] = in_d[...]
        keep[1] = out_d[...]

    @pl.when(jnp.logical_not(is_left))
    def _():
        @pl.when(is_middle)
        def _():
            keep[1] = out_d[...]

        @pl.when(jnp.logical_not(is_middle))
        def _():
            send_d().wait_recv()
            keep[1] = in_d[...]

        @pl.when(is_outer)
        def _():
            keep[0] = jnp.zeros(shape, jnp.float32)

        @pl.when(jnp.logical_not(is_outer))
        def _():
            following = keep[14] - nn(keep[13], keep[1])
            keep[0] = following
            out_d[...] = following
            send_d().start()

    @pl.when(jnp.logical_not(is_middle))
    def _():
        send_b(0).wait_send()
        send_b(1).wait_send()

    x0, xt = keep[1], keep[0]
    xb = keep[10] - nn(keep[8], x0) - nn(keep[9], xt)
    xa = keep[3] - nn(keep[2], x0) - nn(keep[4], xb)
    xd = keep[7] - nn(keep[5], xt) - nn(keep[6], xb)
    blocks = [
        x0, jnp.where(three, xa, xb), jnp.where(three, xb, zero), jnp.where(four, xd, zero)
    ]
    for j in range(cap):
        for i in range(ne):
            out_e[i, j * rows : (j + 1) * rows, :] = blocks[j][i * rows : (i + 1) * rows, :]

    def send_e(i):
        to = lax.rem(e + i, ne)
        return pltpu.make_async_remote_copy(
            src_ref=out_e.at[to], dst_ref=in_e.at[e], send_sem=se.at[i], recv_sem=re.at[i],
            device_id=(to, p), device_id_type=MESH,
        )

    for i in range(1, ne):
        send_e(i).start()
    for j in range(cap):
        lesser[0, j] = blocks[j]
    in_e[e] = out_e[e]

    def weights_of(k, carry):
        here = energies[k].astype(jnp.float32)
        for f in range(ne):
            t = jnp.full((8, 128), energies[f].astype(jnp.float32) - here, jnp.float32)
            weights[k, f] = 0.5 * (
                1.6 * jnp.exp(-((t - 6.0) ** 2) / 18.0) + 0.6 * jnp.exp(-((t + 6.0) ** 2) / 18.0)
            )
        return carry

    lax.fori_loop(0, ne, weights_of, 0)
    for i in range(1, ne):
        send_e(i).wait_recv()

    def row_of(k, carry):
        terms = [weights[k, f][:1] * in_e[f] for f in range(ne)]
        while len(terms) > 1:
            pairs = [terms[i : i + 2] for i in range(0, len(terms), 2)]
            terms = [q[0] + q[1] if len(q) == 2 else q[0] for q in pairs]
        for j in range(cap):
            selfe[k, j] = terms[0][j * rows : (j + 1) * rows, :]
        return carry

    lax.fori_loop(0, ne, row_of, 0)
    for i in range(1, ne):
        send_e(i).wait_send()

    @pl.when(is_left)
    def _():
        send_a(0).wait_send()
        send_a(1).wait_send()

    @pl.when(p == half - 1)
    def _():
        send_a(2).wait_send()

    @pl.when(jnp.logical_not(is_outer))
    def _():
        send_d().wait_send()


def short_kernel(
    ne, nslab, counts_in, energies_in, ham_in, link_in, inj_in, lesser, selfe,
    counts, energies, ham, link, inj, si,
    keep, back, here, there, out_e, in_e, weights, ss, rs, se, re,
):
    pairs = [
        (counts_in, counts), (energies_in, energies), (ham_in, ham), (link_in, link), (inj_in, inj)
    ]
    staged = [pltpu.make_async_copy(a, b, si.at[i]) for i, (a, b) in enumerate(pairs)]
    for copy in staged:
        copy.start()
    e = lax.axis_index("energy")
    p = lax.axis_index("slab")
    width = ham.shape[1]
    cap = ham.shape[0]
    rows = width // ne
    last = nslab - 1
    is_outer = (p == 0) | (p == last)
    is_left = p < 2
    near = jnp.where(is_left, 1 - p, 5 - p)
    middle = jnp.where(is_left, 2, 1)
    far = last - p

    barrier = pltpu.get_barrier_semaphore()
    for i in range(1, ne):
        pl.semaphore_signal(
            barrier, inc=1, device_id=(lax.rem(e + i, ne), p), device_id_type=MESH
        )
    for i in range(1, nslab):
        pl.semaphore_signal(
            barrier, inc=1, device_id=(e, lax.rem(p + i, nslab)), device_id_type=MESH
        )

    C, N, K, R, A0, A1, S0, S1, X, Y, D0, D1 = range(12)

    def send(what, slot, to):
        return pltpu.make_async_remote_copy(
            src_ref=here.at[what], dst_ref=there.at[what],
            send_sem=ss.at[slot], recv_sem=rs.at[what],
            device_id=(e, to), device_id_type=MESH,
        )

    def arrived(what):
        send(what, what, near).wait_recv()

    def from_inner():
        return [send(N, N, near), send(K, K, near), send(R, R, near)]

    def from_second():
        return [send(A0, A0, 2), send(A1, A1, 2)]

    def from_third(i):
        return [send(S0 + i, 12 + 3 * i + j, to) for j, to in enumerate((0, 1, last))]

    def from_outer(i):
        return [
            send(D0 + i, 18 + 2 * i, far), send(D0 + i, 19 + 2 * i, middle), send(X + i, X + i, near)
        ]

    for copy in staged[:3]:
        copy.wait()
    shape = (width, width)
    eye = (
        lax.broadcasted_iota(jnp.int32, shape, 0) == lax.broadcasted_iota(jnp.int32, shape, 1)
    ).astype(jnp.float32)
    shift = 0.02 + 0.06 * energies[e].astype(jnp.float32) / (4 * ne)
    shifted = eye * shift
    at = jnp.full(shape, p, jnp.int32)
    third, inner = at == 2, at < last
    count = jnp.full(shape, counts[p], jnp.int32) - third.astype(jnp.int32)
    one, two, three, four = count == 1, count == 2, count >= 3, count == 4
    zero = jnp.zeros(shape, jnp.float32)

    def ending(blocks):
        return jnp.where(one, blocks[1], jnp.where(two, blocks[2], blocks[3]))

    diag_a = jnp.where(three, ham[1] + shifted, eye)
    diag_d = jnp.where(four, ham[3] + shifted, eye)
    inv_a, inv_d = inverses([diag_a, diag_d])
    for copy in staged[3:]:
        copy.wait()
    here[C] = ending(link).T
    link_0a = jnp.where(three, link[0], zero)
    link_0b = jnp.where(two, link[0], zero)
    link_0t = jnp.where(one, link[0], zero)
    link_ab = jnp.where(three, link[1], zero)
    link_bd = jnp.where(four, link[2], zero)
    link_dt = jnp.where(four & inner, link[3], zero)
    link_bt = jnp.where(two & inner, link[1], jnp.where((count == 3) & inner, link[2], zero))
    rhs_a = jnp.where(three, inj[0, 1], zero)
    rhs_b = jnp.where(three, inj[0, 2], jnp.where(two, inj[0, 1], zero))
    rhs_d = jnp.where(four, inj[0, 3], zero)
    diag_b = jnp.where(three, ham[2] + shifted, jnp.where(two, ham[1] + shifted, eye))

    xab = nn(inv_a, link_ab)
    xdb = nt(inv_d, link_bd)
    diag_b = diag_b - tn(link_ab, xab) - nn(link_bd, xdb)
    keep[2] = inv_a
    keep[3] = inv_d
    keep[4] = xab
    keep[6] = xdb
    pl.semaphore_wait(barrier, ne + nslab - 2)

    @pl.when(p == 2)
    def _():
        send(C, C, last).start()

    inv_a, inv_d, xab, xdb = keep[2], keep[3], keep[4], keep[6]
    xaf = nn(inv_a, rhs_a)
    xdf = nn(inv_d, rhs_d)
    rhs_b = rhs_b - tn(link_ab, xaf) - nn(link_bd, xdf)
    (inv_b,) = inverses([diag_b])
    link_0b = link_0b - nn(link_0a, xab)
    xa0 = nt(inv_a, link_0a)
    xdt = nn(inv_d, link_dt)
    link_bt = link_bt - nn(link_bd, xdt)
    xb0 = nt(inv_b, link_0b)
    xbt = nn(inv_b, link_bt)
    node = ham[0] + shifted - nn(link_0a, xa0) - nn(link_0b, xb0)
    ahead = tn(link_dt, xdt) + tn(link_bt, xbt)
    keep[0] = node
    here[A0] = ahead
    here[N] = jnp.where(third, ending(ham) + shifted - ahead, node)

    @pl.when(jnp.logical_not(is_outer))
    def _():
        from_inner()[0].start()

    @pl.when(p == 1)
    def _():
        from_second()[0].start()

    own_link = link_0t - nn(link_0b, xbt)
    here[K] = jnp.where(third, own_link.T, own_link)
    keep[2] = xa0
    keep[5] = xdt
    keep[8] = xb0
    keep[9] = xbt
    keep[3], keep[7], keep[10] = xaf, xdf, rhs_b
    keep[11] = inv_b
    keep[12] = link_0b
    keep[13] = inj[0, 0] - nn(link_0a, xaf)
    keep[14] = tn(link_dt, xdf)
    keep[15] = link_bt

    def right_sides():
        xbf = nn(keep[11], keep[10])
        node_rhs = keep[13] - nn(keep[12], xbf)
        ahead = keep[14] + tn(keep[15], xbf)
        keep[1] = node_rhs
        keep[10] = xbf
        here[A1] = ahead
        here[R] = jnp.where(third, ending(inj.at[0]) - ahead, node_rhs)

    @pl.when(jnp.logical_not(is_outer))
    def _():
        from_inner()[1].start()

    @pl.when(jnp.logical_not(is_outer))
    def _():
        right_sides()
        from_inner()[2].start()

    @pl.when(p == 1)
    def _():
        from_second()[1].start()

    @pl.when(p == 2)
    def _():
        arrived(A0)
        here[S0] = keep[0] - there[A0]
        for copy in from_third(0):
            copy.start()
        arrived(A1)
        here[S1] = keep[1] - there[A1]
        for copy in from_third(1):
            copy.start()

    @pl.when(is_outer)
    def _():
        (inv_n,) = inverses([keep[0]])
        right_sides()
        keep[15] = inv_n

        @pl.when(p == 0)
        def _():
            keep[11] = here[K]

        @pl.when(p == last)
        def _():
            arrived(C)
            keep[11] = there[C]

        xj = nn(keep[15], keep[11])
        keep[12] = xj
        arrived(N)
        (inv_m,) = inverses([there[N] - here[A0] - tn(keep[11], xj)])
        keep[14] = inv_m
        xr = nn(keep[15], keep[1])
        keep[13] = xr
        below = here[A1] + tn(keep[11], xr)
        arrived(K)
        x = nn(inv_m, there[K])
        here[X] = x
        here[D0] = tn(there[K], x)
        for copy in from_outer(0):
            copy.start()
        arrived(R)
        y = nn(keep[14], there[R] - below)
        here[Y] = y
        here[D1] = tn(there[K], y)
        for copy in from_outer(1):
            copy.start()
        keep[0] = keep[13] - nn(keep[12], y)
        keep[1] = y
        keep[11] = -nn(keep[12], here[X])
        keep[14] = here[X]

    @pl.when(jnp.logical_not(is_outer))
    def _():
        arrived(X)
        x = there[X]
        here[X] = x
        here[D0] = tn(here[K], x)
        keep[11] = jnp.where(third, -eye, x)
        keep[14] = jnp.where(third, x, -eye)

    @pl.when(p != 2)
    def _():
        arrived(S0)
        here[S0] = there[S0]

    arrived(D0)
    (inv_s,) = inverses([here[S0] - here[D0] - there[D0]])
    keep[15] = inv_s
    g0, gt = keep[11], keep[14]
    gb = -nn(keep[8], g0) - nn(keep[9], gt)
    keep[12] = gb
    keep[13] = -nn(keep[2], g0) - nn(keep[4], gb)
    keep[11] = -nn(keep[5], gt) - nn(keep[6], gb)
    back[0] = g0

    @pl.when(jnp.logical_not(is_outer))
    def _():
        arrived(Y)
        y = there[Y]
        here[D1] = tn(here[K], y)
        keep[0] = jnp.where(third, zero, y)
        keep[1] = jnp.where(third, y, zero)

    @pl.when(p != 2)
    def _():
        arrived(S1)
        here[S1] = there[S1]

    arrived(D1)
    x2 = nn(keep[15], here[S1] - here[D1] - there[D1])
    f0, ft = keep[0], keep[1]
    fb = keep[10] - nn(keep[8], f0) - nn(keep[9], ft)
    fa = keep[3] - nn(keep[2], f0) - nn(keep[4], fb)
    fd = keep[7] - nn(keep[5], ft) - nn(keep[6], fb)
    x0 = f0 - nn(back[0], x2)
    xt = ft - nn(keep[14], x2)
    xb = fb - nn(keep[12], x2)
    xa = fa - nn(keep[13], x2)
    xd = fd - nn(keep[11], x2)
    blocks = [
        x0,
        jnp.where(three, xa, jnp.where(one, xt, xb)),
        jnp.where(three, xb, jnp.where(two & third, xt, zero)),
        jnp.where(four, xd, jnp.where(three & third, xt, zero)),
    ]
    for j in range(cap):
        for i in range(ne):
            out_e[i, j * rows : (j + 1) * rows, :] = blocks[j][i * rows : (i + 1) * rows, :]

    def send_e(i):
        to = lax.rem(e + i, ne)
        return pltpu.make_async_remote_copy(
            src_ref=out_e.at[to], dst_ref=in_e.at[e], send_sem=se.at[i], recv_sem=re.at[i],
            device_id=(to, p), device_id_type=MESH,
        )

    for i in range(1, ne):
        send_e(i).start()
    for j in range(cap):
        lesser[0, j] = blocks[j]
    in_e[e] = out_e[e]

    def weights_of(k, carry):
        here = energies[k].astype(jnp.float32)
        for f in range(ne):
            t = jnp.full((8, 128), energies[f].astype(jnp.float32) - here, jnp.float32)
            weights[k, f] = 0.5 * (
                1.6 * jnp.exp(-((t - 6.0) ** 2) / 18.0) + 0.6 * jnp.exp(-((t + 6.0) ** 2) / 18.0)
            )
        return carry

    lax.fori_loop(0, ne, weights_of, 0)
    for i in range(1, ne):
        send_e(i).wait_recv()

    def row_of(k, carry):
        terms = [weights[k, f][:1] * in_e[f] for f in range(ne)]
        while len(terms) > 1:
            pairs = [terms[i : i + 2] for i in range(0, len(terms), 2)]
            terms = [q[0] + q[1] if len(q) == 2 else q[0] for q in pairs]
        for j in range(cap):
            selfe[k, j] = terms[0][j * rows : (j + 1) * rows, :]
        return carry

    lax.fori_loop(0, ne, row_of, 0)
    for i in range(1, ne):
        send_e(i).wait_send()

    @pl.when(jnp.logical_not(is_outer))
    def _():
        for copy in from_inner():
            copy.wait_send()

    @pl.when(is_outer)
    def _():
        for copy in from_outer(0) + from_outer(1):
            copy.wait_send()

    @pl.when(p == 1)
    def _():
        for copy in from_second():
            copy.wait_send()

    @pl.when(p == 2)
    def _():
        for copy in [send(C, C, last)] + from_third(0) + from_third(1):
            copy.wait_send()


def hand_over(*arrays):
    def move(*refs):
        for source, result in zip(refs, refs[len(arrays) :]):
            result[...] = source[...]

    vmem = pl.BlockSpec(memory_space=pltpu.VMEM)
    return pl.pallas_call(
        move,
        out_shape=tuple(jax.ShapeDtypeStruct(a.shape, a.dtype) for a in arrays),
        in_specs=[vmem] * len(arrays),
        out_specs=(vmem,) * len(arrays),
    )(*arrays)


def per_device(ne, nslab, counts, energies, ham, link, inj):
    cap, width, _ = ham.shape
    rows = width // ne
    block = lambda *n: pltpu.VMEM((*n, width, width), jnp.float32)
    dma = pltpu.SemaphoreType.DMA
    vmem = pl.BlockSpec(memory_space=pltpu.VMEM)
    hbm = pl.BlockSpec(memory_space=pltpu.HBM)
    exchange = pltpu.VMEM((ne, cap * rows, width), jnp.float32)
    staging = [
        pltpu.SMEM(counts.shape, jnp.int32), pltpu.SMEM(energies.shape, jnp.int32),
        pltpu.VMEM(ham.shape, jnp.float32), pltpu.VMEM(link.shape, jnp.float32),
        pltpu.VMEM(inj.shape, jnp.float32), dma((5,)),
    ]
    last = [exchange, exchange, pltpu.VMEM((ne, ne, 8, 128), jnp.float32)]
    if nslab == 4:
        body = short_kernel
        scratch = [block(16), block(1), block(12), block(12), *last, dma((22,)), dma((12,))]
    else:
        body = kernel
        scratch = [
            block(16), block(3), block(3), block(2), block(2), block(2), block(2), block(), block(),
            *last, dma((3,)), dma((3,)), dma((2,)), dma((2,)), dma((2,)), dma((2,)), dma, dma,
        ]
    results = pl.pallas_call(
        functools.partial(body, ne, nslab),
        out_shape=(
            jax.ShapeDtypeStruct(inj.shape, jnp.float32),
            jax.ShapeDtypeStruct((ne, cap, rows, width), jnp.float32),
        ),
        in_specs=[hbm] * 5,
        out_specs=(vmem, vmem),
        scratch_shapes=[*staging, *scratch, dma((ne,)), dma((ne,))],
        compiler_params=pltpu.CompilerParams(
            collective_id=0, has_side_effects=True, vmem_limit_bytes=62 << 20
        ),
    )(counts, energies, ham, link, inj)
    return hand_over(*results)


def solution(mesh):
    return jax.shard_map(
        functools.partial(per_device, mesh.shape["energy"], mesh.shape["slab"]),
        mesh=mesh,
        in_specs=(
            P(),
            P(),
            P("slab", None, None),
            P("slab", None, None),
            P("energy", "slab", None, None),
        ),
        out_specs=(P("energy", "slab", None, None), P(None, "slab", "energy", None)),
        check_vma=False,
    )
```

```python
import functools
import jax
import jax.numpy as jnp
from jax import lax
from jax.experimental import pallas as pl
from jax.experimental.pallas import tpu as pltpu
from jax.sharding import PartitionSpec as P

HIGHEST = lax.Precision.HIGHEST
MESH = pl.DeviceIdType.MESH


def contract(left, right, a, b):
    return lax.dot_general(
        left, right, (((a,), (b,)), ((), ())), precision=HIGHEST, preferred_element_type=jnp.float32
    )


def nn(left, right):
    return contract(left, right, 1, 0)


def tn(left, right):
    return contract(left, right, 0, 0)


def nt(left, right):
    return contract(left, right, 1, 1)


def spread(x, q):
    return jnp.broadcast_to(x[q : q + 1, :], (8, 128))


def across(x, k):
    return jnp.take_along_axis(x, jnp.full((8, 128), k, jnp.int32), axis=1)


def tree(terms):
    while len(terms) > 1:
        terms = [terms[i] + terms[i + 1] for i in range(0, len(terms), 2)]
    return terms[0]


def pivot_rows(rows, columns, sub):
    for q in range(0, 8, 2):
        first, both = sub == q, (sub == q) | (sub == q + 1)
        x, y = columns[q], columns[q + 1]
        a, b, d = spread(x, q), spread(y, q), spread(y, q + 1)
        inv = 1.0 / (a * d - b * b)
        gx = jnp.where(both, jnp.where(first, -1.0, 0.0), x)
        gy = jnp.where(both, jnp.where(first, 0.0, -1.0), y)
        fx = d * gx - b * gy
        fy = a * gy - b * gx
        ex, ey = fx * inv, fy * inv
        for j in range(q + 2, 8):
            u, v = spread(columns[j], q), spread(columns[j], q + 1)
            rest = jnp.where(both, 0.0, columns[j])
            change = (fx * u + fy * v) * inv if j < q + 4 else ex * u + ey * v
            columns[j] = rest - change
        change = ex * spread(rows, q) + ey * spread(rows, q + 1)
        rows = jnp.where(both, 0.0, rows) - change
    return rows


def sweep(chunks, at, k, lane, sub):
    columns = [[across(c, k + q) for c in chunks] for q in range(8)]
    inside = (lane >= k) & (lane < k + 8)
    pivots = jnp.where(inside, jnp.where(lane - k == sub, -1.0, 0.0), chunks[at])
    solved = pivot_rows(pivots, [column[at] for column in columns], sub)
    rows = [spread(solved, q) for q in range(8)]
    out = []
    for c in range(len(chunks)):
        if c == at:
            out.append(solved)
        else:
            change = tree([columns[q][c] * rows[q] for q in range(8)])
            out.append(jnp.where(inside, 0.0, chunks[c]) - change)
    return out


def inverses(matrices):
    width = matrices[0].shape[0]
    size = width // 2 if len(matrices) == 1 else width // 4
    lane = lax.broadcasted_iota(jnp.int32, (8, 128), 1)
    sub = lax.broadcasted_iota(jnp.int32, (8, 128), 0)
    count = width // 8
    sets = [[m[8 * i : 8 * i + 8, :] for i in range(count)] for m in matrices]
    for start in range(0, width, size):
        low, high = start // 8, (start + size) // 8
        panels = [s[low:high] for s in sets]
        for g in range(high - low):
            panels = [sweep(p, g, start + 8 * g, lane, sub) for p in panels]
        for i in range(len(sets)):
            rest = jnp.concatenate(sets[i][:low] + sets[i][high:], axis=0)
            zero = jnp.zeros((8, width), jnp.float32)
            panel = jnp.concatenate([zero] * low + panels[i] + [zero] * (count - high), axis=0)
            column = lax.broadcasted_iota(jnp.int32, rest.shape, 1)
            inside = (column >= start) & (column < start + size)
            rest = jnp.where(inside, 0.0, rest) - nn(rest, panel)
            rest = [rest[8 * j : 8 * j + 8, :] for j in range(count - high + low)]
            sets[i] = rest[:low] + panels[i] + rest[low:]
    return [-jnp.concatenate(s, axis=0) for s in sets]


def kernel(
    ne, nslab, counts_in, energies_in, ham_in, link_in, inj_in, lesser, selfe,
    counts, energies, ham, link, inj, si,
    keep, out_a, in_a, out_b, in_b, out_c, in_c, out_d, in_d, out_e, in_e, weights,
    sa, ra, sb, rb, sc, rc, sd, rd, se, re,
):
    pairs = [
        (counts_in, counts), (energies_in, energies), (ham_in, ham), (link_in, link), (inj_in, inj)
    ]
    staged = [pltpu.make_async_copy(a, b, si.at[i]) for i, (a, b) in enumerate(pairs)]
    for copy in staged:
        copy.start()
    e = lax.axis_index("energy")
    p = lax.axis_index("slab")
    half = nslab // 2
    width = ham.shape[1]
    cap = ham.shape[0]
    rows = width // ne
    is_left = p < half
    is_outer = (p == 0) | (p == nslab - 1)
    is_middle = (p == half - 1) | (p == half)
    takes_a = (p > 0) & (p <= half)
    inward = jnp.where(is_left, p + 1, p - 1)
    outward = jnp.where(is_left, p - 1, p + 1)

    barrier = pltpu.get_barrier_semaphore()
    for i in range(1, ne):
        pl.semaphore_signal(
            barrier, inc=1, device_id=(lax.rem(e + i, ne), p), device_id_type=MESH
        )

    @pl.when(p > 0)
    def _():
        pl.semaphore_signal(barrier, inc=1, device_id=(e, p - 1), device_id_type=MESH)

    @pl.when(p < nslab - 1)
    def _():
        pl.semaphore_signal(barrier, inc=1, device_id=(e, p + 1), device_id_type=MESH)

    def send(src, dst, send_sem, recv_sem, to):
        return pltpu.make_async_remote_copy(
            src_ref=src, dst_ref=dst, send_sem=send_sem, recv_sem=recv_sem,
            device_id=(e, to), device_id_type=MESH,
        )

    for copy in staged:
        copy.wait()
    shape = (width, width)
    eye = (
        lax.broadcasted_iota(jnp.int32, shape, 0) == lax.broadcasted_iota(jnp.int32, shape, 1)
    ).astype(jnp.float32)
    shift = 0.02 + 0.06 * energies[e].astype(jnp.float32) / (4 * ne)
    shifted = eye * shift
    count = jnp.full(shape, counts[p], jnp.int32)
    two, three, four = count == 2, count >= 3, count == 4
    inner = jnp.full(shape, p, jnp.int32) < nslab - 1
    zero = jnp.zeros(shape, jnp.float32)

    diag_a = jnp.where(three, ham[1] + shifted, eye)
    diag_d = jnp.where(four, ham[3] + shifted, eye)
    inv_a, inv_d = inverses([diag_a, diag_d])
    link_0a = jnp.where(three, link[0], zero)
    link_0b = jnp.where(three, zero, link[0])
    link_ab = jnp.where(three, link[1], zero)
    link_bd = jnp.where(four, link[2], zero)
    link_dt = jnp.where(four & inner, link[3], zero)
    link_bt = jnp.where(inner, jnp.where(two, link[1], jnp.where(four, zero, link[2])), zero)
    rhs_a = jnp.where(three, inj[0, 1], zero)
    rhs_b = jnp.where(three, inj[0, 2], inj[0, 1])
    rhs_d = jnp.where(four, inj[0, 3], zero)
    diag_b = jnp.where(three, ham[2], ham[1]) + shifted

    xab = nn(inv_a, link_ab)
    xdb = nt(inv_d, link_bd)
    diag_b = diag_b - tn(link_ab, xab) - nn(link_bd, xdb)
    keep[2] = inv_a
    keep[3] = inv_d
    keep[4] = xab
    keep[6] = xdb
    (inv_b,) = inverses([diag_b])

    def send_a(i):
        return send(out_a.at[i], in_a.at[i], sa.at[i], ra.at[i], p + 1)

    def send_b(i):
        return send(out_b.at[i], in_b.at[i], sb.at[i], rb.at[i], inward)

    def send_c(i):
        return send(out_c.at[i], in_c.at[i], sc.at[i], rc.at[i], inward)

    def send_d():
        return send(out_d, in_d, sd, rd, outward)

    inv_a, inv_d, xab, xdb = keep[2], keep[3], keep[4], keep[6]
    link_0b = link_0b - nn(link_0a, xab)
    xa0 = nt(inv_a, link_0a)
    xb0 = nt(inv_b, link_0b)
    node = ham[0] + shifted - nn(link_0a, xa0) - nn(link_0b, xb0)
    keep[0] = node
    out_b[0] = node
    keep[2] = xa0
    keep[8] = xb0

    pl.semaphore_wait(barrier, ne - 1 + jnp.where(is_outer, 1, 2))

    @pl.when(p == nslab - 1)
    def _():
        send_b(0).start()

    xdt = nn(inv_d, link_dt)
    link_bt = link_bt - nn(link_bd, xdt)
    xbt = nn(inv_b, link_bt)
    out_a[0] = tn(link_dt, xdt) + tn(link_bt, xbt)
    keep[5] = xdt
    keep[9] = xbt

    @pl.when(is_left)
    def _():
        send_a(0).start()

    xaf = nn(inv_a, rhs_a)
    xdf = nn(inv_d, rhs_d)
    rhs_b = rhs_b - tn(link_ab, xaf) - nn(link_bd, xdf)
    xbf = nn(inv_b, rhs_b)
    node_rhs = inj[0, 0] - nn(link_0a, xaf) - nn(link_0b, xbf)
    keep[1] = node_rhs
    out_b[1] = node_rhs

    @pl.when(p == nslab - 1)
    def _():
        send_b(1).start()

    out_a[1] = tn(link_dt, xdf) + tn(link_bt, xbf)
    out_a[2] = -tn(link_bt, xb0)

    @pl.when(is_left)
    def _():
        send_a(1).start()

    @pl.when(p == half - 1)
    def _():
        send_a(2).start()

    own_link = -nn(link_0b, xbt)
    keep[3], keep[7], keep[10] = xaf, xdf, xbf
    keep[11] = own_link
    keep[12] = own_link

    @pl.when(jnp.logical_not(is_left) & jnp.logical_not(is_outer))
    def _():
        send_b(0).wait_recv()
        (inv_t,) = inverses([in_b[0] - out_a[0]])
        xj = nt(inv_t, keep[11])
        keep[0] = keep[0] - nn(keep[11], xj)
        send_b(1).wait_recv()
        xr = nn(inv_t, in_b[1] - out_a[1])
        keep[1] = keep[1] - nn(keep[11], xr)
        keep[13] = xj
        keep[14] = xr

        @pl.when(jnp.logical_not(is_middle))
        def _():
            out_b[0] = keep[0]
            send_b(0).start()
            out_b[1] = keep[1]
            send_b(1).start()

    @pl.when(takes_a)
    def _():
        send_a(0).wait_recv()
        send_a(1).wait_recv()
        keep[0] = keep[0] - in_a[0]
        keep[1] = keep[1] - in_a[1]

    @pl.when(is_left & jnp.logical_not(is_outer))
    def _():
        send_b(0).wait_recv()
        keep[0] = keep[0] - in_b[0]

    @pl.when(is_left | is_middle)
    def _():
        (inv_n,) = inverses([keep[0]])
        keep[15] = inv_n

    @pl.when(is_left & jnp.logical_not(is_outer))
    def _():
        send_b(1).wait_recv()
        keep[1] = keep[1] - in_b[1]

    @pl.when(is_middle & jnp.logical_not(is_left))
    def _():
        send_a(2).wait_recv()
        keep[12] = in_a[2]

    @pl.when(is_middle)
    def _():
        inv_n = keep[15]
        out_c[0] = nn(inv_n, keep[12])
        send_c(0).start()
        out_c[1] = nn(inv_n, keep[1])
        send_c(1).start()
        send_c(0).wait_recv()
        (inv_m,) = inverses([keep[0] - nn(keep[12], in_c[0])])
        send_c(1).wait_recv()
        x0 = nn(inv_m, keep[1] - nn(keep[12], in_c[1]))
        out_d[...] = x0

        @pl.when(is_left & jnp.logical_not(is_outer))
        def _():
            send_d().start()

        in_d[...] = in_c[1] - nn(in_c[0], x0)
        send_c(0).wait_send()
        send_c(1).wait_send()

    @pl.when(is_left & jnp.logical_not(is_middle))
    def _():
        inv_n = keep[15]
        xj = nn(inv_n, keep[12])
        out_b[0] = tn(keep[12], xj)
        send_b(0).start()
        xr = nn(inv_n, keep[1])
        out_b[1] = tn(keep[12], xr)
        send_b(1).start()
        send_d().wait_recv()
        out_d[...] = xr - nn(xj, in_d[...])

    @pl.when(is_left & jnp.logical_not(is_outer) & jnp.logical_not(is_middle))
    def _():
        send_d().start()

    @pl.when(is_left)
    def _():
        keep[0] = in_d[...]
        keep[1] = out_d[...]

    @pl.when(jnp.logical_not(is_left))
    def _():
        @pl.when(is_middle)
        def _():
            keep[1] = out_d[...]

        @pl.when(jnp.logical_not(is_middle))
        def _():
            send_d().wait_recv()
            keep[1] = in_d[...]

        @pl.when(is_outer)
        def _():
            keep[0] = jnp.zeros(shape, jnp.float32)

        @pl.when(jnp.logical_not(is_outer))
        def _():
            following = keep[14] - nn(keep[13], keep[1])
            keep[0] = following
            out_d[...] = following
            send_d().start()

    @pl.when(jnp.logical_not(is_middle))
    def _():
        send_b(0).wait_send()
        send_b(1).wait_send()

    x0, xt = keep[1], keep[0]
    xb = keep[10] - nn(keep[8], x0) - nn(keep[9], xt)
    xa = keep[3] - nn(keep[2], x0) - nn(keep[4], xb)
    xd = keep[7] - nn(keep[5], xt) - nn(keep[6], xb)
    blocks = [
        x0, jnp.where(three, xa, xb), jnp.where(three, xb, zero), jnp.where(four, xd, zero)
    ]
    for j in range(cap):
        for i in range(ne):
            out_e[i, j * rows : (j + 1) * rows, :] = blocks[j][i * rows : (i + 1) * rows, :]

    def send_e(i):
        to = lax.rem(e + i, ne)
        return pltpu.make_async_remote_copy(
            src_ref=out_e.at[to], dst_ref=in_e.at[e], send_sem=se.at[i], recv_sem=re.at[i],
            device_id=(to, p), device_id_type=MESH,
        )

    for i in range(1, ne):
        send_e(i).start()
    for j in range(cap):
        lesser[0, j] = blocks[j]
    in_e[e] = out_e[e]

    def weights_of(k, carry):
        here = energies[k].astype(jnp.float32)
        for f in range(ne):
            t = jnp.full((8, 128), energies[f].astype(jnp.float32) - here, jnp.float32)
            weights[k, f] = 0.5 * (
                1.6 * jnp.exp(-((t - 6.0) ** 2) / 18.0) + 0.6 * jnp.exp(-((t + 6.0) ** 2) / 18.0)
            )
        return carry

    lax.fori_loop(0, ne, weights_of, 0)
    for i in range(1, ne):
        send_e(i).wait_recv()

    def row_of(k, carry):
        terms = [weights[k, f][:1] * in_e[f] for f in range(ne)]
        while len(terms) > 1:
            pairs = [terms[i : i + 2] for i in range(0, len(terms), 2)]
            terms = [q[0] + q[1] if len(q) == 2 else q[0] for q in pairs]
        for j in range(cap):
            selfe[k, j] = terms[0][j * rows : (j + 1) * rows, :]
        return carry

    lax.fori_loop(0, ne, row_of, 0)
    for i in range(1, ne):
        send_e(i).wait_send()

    @pl.when(is_left)
    def _():
        send_a(0).wait_send()
        send_a(1).wait_send()

    @pl.when(p == half - 1)
    def _():
        send_a(2).wait_send()

    @pl.when(jnp.logical_not(is_outer))
    def _():
        send_d().wait_send()


def halves(x):
    high = x.astype(jnp.bfloat16)
    return high, (x - high.astype(jnp.float32)).astype(jnp.bfloat16)


def product(left, right, a, b):
    dims = (((a,), (b,)), ((), ()))
    dot = lambda x, y: lax.dot_general(x, y, dims, preferred_element_type=jnp.float32)
    (lh, ll), (rh, rl) = halves(left), halves(right)
    return dot(lh, rh) + (dot(lh, rl) + dot(ll, rh))


def nn3(left, right):
    return product(left, right, 1, 0)


def tn3(left, right):
    return product(left, right, 0, 0)


def nt3(left, right):
    return product(left, right, 1, 1)


def short_kernel(
    ne, nslab, counts_in, energies_in, ham_in, link_in, inj_in, lesser, selfe,
    counts, energies, ham, link, inj, si,
    keep, back, here, there, out_e, in_e, weights, ss, rs, se, re,
):
    pairs = [
        (counts_in, counts), (energies_in, energies), (ham_in, ham), (link_in, link), (inj_in, inj)
    ]
    staged = [pltpu.make_async_copy(a, b, si.at[i]) for i, (a, b) in enumerate(pairs)]
    for copy in staged:
        copy.start()
    e = lax.axis_index("energy")
    p = lax.axis_index("slab")
    width = ham.shape[1]
    cap = ham.shape[0]
    rows = width // ne
    last = nslab - 1
    is_outer = (p == 0) | (p == last)
    is_left = p < 2
    near = jnp.where(is_left, 1 - p, 5 - p)
    middle = jnp.where(is_left, 2, 1)
    far = last - p

    barrier = pltpu.get_barrier_semaphore()
    for i in range(1, ne):
        pl.semaphore_signal(
            barrier, inc=1, device_id=(lax.rem(e + i, ne), p), device_id_type=MESH
        )
    for i in range(1, nslab):
        pl.semaphore_signal(
            barrier, inc=1, device_id=(e, lax.rem(p + i, nslab)), device_id_type=MESH
        )

    C, N, K, R, A0, A1, S0, S1, X, Y, D0, D1 = range(12)

    def send(what, slot, to):
        return pltpu.make_async_remote_copy(
            src_ref=here.at[what], dst_ref=there.at[what],
            send_sem=ss.at[slot], recv_sem=rs.at[what],
            device_id=(e, to), device_id_type=MESH,
        )

    def arrived(what):
        send(what, what, near).wait_recv()

    def from_inner():
        return [send(N, N, near), send(K, K, near), send(R, R, near)]

    def from_second():
        return [send(A0, A0, 2), send(A1, A1, 2)]

    def from_third(i):
        return [send(S0 + i, 12 + 3 * i + j, to) for j, to in enumerate((0, 1, last))]

    def from_outer(i):
        return [
            send(D0 + i, 18 + 2 * i, far), send(D0 + i, 19 + 2 * i, middle), send(X + i, X + i, near)
        ]

    for copy in staged[:3]:
        copy.wait()
    shape = (width, width)
    eye = (
        lax.broadcasted_iota(jnp.int32, shape, 0) == lax.broadcasted_iota(jnp.int32, shape, 1)
    ).astype(jnp.float32)
    shift = 0.02 + 0.06 * energies[e].astype(jnp.float32) / (4 * ne)
    shifted = eye * shift
    at = jnp.full(shape, p, jnp.int32)
    third, inner = at == 2, at < last
    count = jnp.full(shape, counts[p], jnp.int32) - third.astype(jnp.int32)
    one, two, three, four = count == 1, count == 2, count >= 3, count == 4
    zero = jnp.zeros(shape, jnp.float32)

    def ending(blocks):
        return jnp.where(one, blocks[1], jnp.where(two, blocks[2], blocks[3]))

    diag_a = jnp.where(three, ham[1] + shifted, eye)
    diag_d = jnp.where(four, ham[3] + shifted, eye)
    inv_a, inv_d = inverses([diag_a, diag_d])
    for copy in staged[3:]:
        copy.wait()
    here[C] = ending(link).T
    link_0a = jnp.where(three, link[0], zero)
    link_0b = jnp.where(two, link[0], zero)
    link_0t = jnp.where(one, link[0], zero)
    link_ab = jnp.where(three, link[1], zero)
    link_bd = jnp.where(four, link[2], zero)
    link_dt = jnp.where(four & inner, link[3], zero)
    link_bt = jnp.where(two & inner, link[1], jnp.where((count == 3) & inner, link[2], zero))
    rhs_a = jnp.where(three, inj[0, 1], zero)
    rhs_b = jnp.where(three, inj[0, 2], jnp.where(two, inj[0, 1], zero))
    rhs_d = jnp.where(four, inj[0, 3], zero)
    diag_b = jnp.where(three, ham[2] + shifted, jnp.where(two, ham[1] + shifted, eye))

    xab = nn(inv_a, link_ab)
    xdb = nt(inv_d, link_bd)
    diag_b = diag_b - tn(link_ab, xab) - nn(link_bd, xdb)
    keep[2] = inv_a
    keep[3] = inv_d
    keep[4] = xab
    keep[6] = xdb
    pl.semaphore_wait(barrier, ne + nslab - 2)

    @pl.when(p == 2)
    def _():
        send(C, C, last).start()

    inv_a, inv_d, xab, xdb = keep[2], keep[3], keep[4], keep[6]
    xaf = nn(inv_a, rhs_a)
    xdf = nn(inv_d, rhs_d)
    rhs_b = rhs_b - tn(link_ab, xaf) - nn(link_bd, xdf)
    (inv_b,) = inverses([diag_b])
    link_0b = link_0b - nn(link_0a, xab)
    xa0 = nt(inv_a, link_0a)
    xdt = nn(inv_d, link_dt)
    link_bt = link_bt - nn(link_bd, xdt)
    xb0 = nt(inv_b, link_0b)
    xbt = nn(inv_b, link_bt)
    node = ham[0] + shifted - nn(link_0a, xa0) - nn(link_0b, xb0)
    ahead = tn(link_dt, xdt) + tn(link_bt, xbt)
    keep[0] = node
    here[A0] = ahead
    here[N] = jnp.where(third, ending(ham) + shifted - ahead, node)

    @pl.when(jnp.logical_not(is_outer))
    def _():
        from_inner()[0].start()

    @pl.when(p == 1)
    def _():
        from_second()[0].start()

    own_link = link_0t - nn(link_0b, xbt)
    here[K] = jnp.where(third, own_link.T, own_link)
    keep[2] = xa0
    keep[5] = xdt
    keep[8] = xb0
    keep[9] = xbt
    keep[3], keep[7], keep[10] = xaf, xdf, rhs_b
    keep[11] = inv_b
    keep[12] = link_0b
    keep[13] = inj[0, 0] - nn(link_0a, xaf)
    keep[14] = tn(link_dt, xdf)
    keep[15] = link_bt

    def right_sides():
        xbf = nn(keep[11], keep[10])
        node_rhs = keep[13] - nn(keep[12], xbf)
        ahead = keep[14] + tn(keep[15], xbf)
        keep[1] = node_rhs
        keep[10] = xbf
        here[A1] = ahead
        here[R] = jnp.where(third, ending(inj.at[0]) - ahead, node_rhs)

    @pl.when(jnp.logical_not(is_outer))
    def _():
        from_inner()[1].start()

    @pl.when(jnp.logical_not(is_outer))
    def _():
        right_sides()
        from_inner()[2].start()

    @pl.when(p == 1)
    def _():
        from_second()[1].start()

    @pl.when(p == 2)
    def _():
        arrived(A0)
        here[S0] = keep[0] - there[A0]
        for copy in from_third(0):
            copy.start()
        arrived(A1)
        here[S1] = keep[1] - there[A1]
        for copy in from_third(1):
            copy.start()

    @pl.when(is_outer)
    def _():
        (inv_n,) = inverses([keep[0]])
        right_sides()
        keep[15] = inv_n

        @pl.when(p == 0)
        def _():
            keep[11] = here[K]

        @pl.when(p == last)
        def _():
            arrived(C)
            keep[11] = there[C]

        xj = nn(keep[15], keep[11])
        keep[12] = xj
        arrived(N)
        (inv_m,) = inverses([there[N] - here[A0] - tn(keep[11], xj)])
        keep[14] = inv_m
        xr = nn(keep[15], keep[1])
        keep[13] = xr
        below = here[A1] + tn(keep[11], xr)
        arrived(K)
        x = nn(inv_m, there[K])
        here[X] = x
        here[D0] = tn(there[K], x)
        for copy in from_outer(0):
            copy.start()
        arrived(R)
        y = nn(keep[14], there[R] - below)
        here[Y] = y
        here[D1] = tn(there[K], y)
        for copy in from_outer(1):
            copy.start()
        keep[0] = keep[13] - nn(keep[12], y)
        keep[1] = y
        keep[11] = -nn(keep[12], here[X])
        keep[14] = here[X]

    @pl.when(jnp.logical_not(is_outer))
    def _():
        arrived(X)
        x = there[X]
        here[X] = x
        here[D0] = tn(here[K], x)
        keep[11] = jnp.where(third, -eye, x)
        keep[14] = jnp.where(third, x, -eye)

    @pl.when(p != 2)
    def _():
        arrived(S0)
        here[S0] = there[S0]

    arrived(D0)
    (inv_s,) = inverses([here[S0] - here[D0] - there[D0]])
    keep[15] = inv_s
    g0, gt = keep[11], keep[14]
    gb = -nn3(keep[8], g0) - nn3(keep[9], gt)
    keep[12] = gb
    keep[13] = -nn3(keep[2], g0) - nn3(keep[4], gb)
    keep[11] = -nn3(keep[5], gt) - nn3(keep[6], gb)
    back[0] = g0

    @pl.when(jnp.logical_not(is_outer))
    def _():
        arrived(Y)
        y = there[Y]
        here[D1] = tn(here[K], y)
        keep[0] = jnp.where(third, zero, y)
        keep[1] = jnp.where(third, y, zero)

    @pl.when(p != 2)
    def _():
        arrived(S1)
        here[S1] = there[S1]

    arrived(D1)
    x2 = nn(keep[15], here[S1] - here[D1] - there[D1])
    f0, ft = keep[0], keep[1]
    fb = keep[10] - nn3(keep[8], f0) - nn3(keep[9], ft)
    fa = keep[3] - nn3(keep[2], f0) - nn3(keep[4], fb)
    fd = keep[7] - nn3(keep[5], ft) - nn3(keep[6], fb)
    x0 = f0 - nn3(back[0], x2)
    xt = ft - nn3(keep[14], x2)
    xb = fb - nn3(keep[12], x2)
    xa = fa - nn3(keep[13], x2)
    xd = fd - nn3(keep[11], x2)
    blocks = [
        x0,
        jnp.where(three, xa, jnp.where(one, xt, xb)),
        jnp.where(three, xb, jnp.where(two & third, xt, zero)),
        jnp.where(four, xd, jnp.where(three & third, xt, zero)),
    ]
    for j in range(cap):
        for i in range(ne):
            out_e[i, j * rows : (j + 1) * rows, :] = blocks[j][i * rows : (i + 1) * rows, :]

    def send_e(i):
        to = lax.rem(e + i, ne)
        return pltpu.make_async_remote_copy(
            src_ref=out_e.at[to], dst_ref=in_e.at[e], send_sem=se.at[i], recv_sem=re.at[i],
            device_id=(to, p), device_id_type=MESH,
        )

    for i in range(1, ne):
        send_e(i).start()
    for j in range(cap):
        lesser[0, j] = blocks[j]
    in_e[e] = out_e[e]

    def weights_of(k, carry):
        here = energies[k].astype(jnp.float32)
        for f in range(ne):
            t = jnp.full((8, 128), energies[f].astype(jnp.float32) - here, jnp.float32)
            weights[k, f] = 0.5 * (
                1.6 * jnp.exp(-((t - 6.0) ** 2) / 18.0) + 0.6 * jnp.exp(-((t + 6.0) ** 2) / 18.0)
            )
        return carry

    lax.fori_loop(0, ne, weights_of, 0)
    for i in range(1, ne):
        send_e(i).wait_recv()

    def row_of(k, carry):
        terms = [weights[k, f][:1] * in_e[f] for f in range(ne)]
        while len(terms) > 1:
            pairs = [terms[i : i + 2] for i in range(0, len(terms), 2)]
            terms = [q[0] + q[1] if len(q) == 2 else q[0] for q in pairs]
        for j in range(cap):
            selfe[k, j] = terms[0][j * rows : (j + 1) * rows, :]
        return carry

    lax.fori_loop(0, ne, row_of, 0)
    for i in range(1, ne):
        send_e(i).wait_send()

    @pl.when(jnp.logical_not(is_outer))
    def _():
        for copy in from_inner():
            copy.wait_send()

    @pl.when(is_outer)
    def _():
        for copy in from_outer(0) + from_outer(1):
            copy.wait_send()

    @pl.when(p == 1)
    def _():
        for copy in from_second():
            copy.wait_send()

    @pl.when(p == 2)
    def _():
        for copy in [send(C, C, last)] + from_third(0) + from_third(1):
            copy.wait_send()


def hand_over(*arrays):
    def move(*refs):
        for source, result in zip(refs, refs[len(arrays) :]):
            result[...] = source[...]

    vmem = pl.BlockSpec(memory_space=pltpu.VMEM)
    return pl.pallas_call(
        move,
        out_shape=tuple(jax.ShapeDtypeStruct(a.shape, a.dtype) for a in arrays),
        in_specs=[vmem] * len(arrays),
        out_specs=(vmem,) * len(arrays),
    )(*arrays)


def per_device(ne, nslab, counts, energies, ham, link, inj):
    cap, width, _ = ham.shape
    rows = width // ne
    block = lambda *n: pltpu.VMEM((*n, width, width), jnp.float32)
    dma = pltpu.SemaphoreType.DMA
    vmem = pl.BlockSpec(memory_space=pltpu.VMEM)
    hbm = pl.BlockSpec(memory_space=pltpu.HBM)
    exchange = pltpu.VMEM((ne, cap * rows, width), jnp.float32)
    staging = [
        pltpu.SMEM(counts.shape, jnp.int32), pltpu.SMEM(energies.shape, jnp.int32),
        pltpu.VMEM(ham.shape, jnp.float32), pltpu.VMEM(link.shape, jnp.float32),
        pltpu.VMEM(inj.shape, jnp.float32), dma((5,)),
    ]
    last = [exchange, exchange, pltpu.VMEM((ne, ne, 8, 128), jnp.float32)]
    if nslab == 4:
        body = short_kernel
        scratch = [block(16), block(1), block(12), block(12), *last, dma((22,)), dma((12,))]
    else:
        body = kernel
        scratch = [
            block(16), block(3), block(3), block(2), block(2), block(2), block(2), block(), block(),
            *last, dma((3,)), dma((3,)), dma((2,)), dma((2,)), dma((2,)), dma((2,)), dma, dma,
        ]
    results = pl.pallas_call(
        functools.partial(body, ne, nslab),
        out_shape=(
            jax.ShapeDtypeStruct(inj.shape, jnp.float32),
            jax.ShapeDtypeStruct((ne, cap, rows, width), jnp.float32),
        ),
        in_specs=[hbm] * 5,
        out_specs=(vmem, vmem),
        scratch_shapes=[*staging, *scratch, dma((ne,)), dma((ne,))],
        compiler_params=pltpu.CompilerParams(
            collective_id=0, has_side_effects=True, vmem_limit_bytes=62 << 20
        ),
    )(counts, energies, ham, link, inj)
    return hand_over(*results)


def solution(mesh):
    return jax.shard_map(
        functools.partial(per_device, mesh.shape["energy"], mesh.shape["slab"]),
        mesh=mesh,
        in_specs=(
            P(),
            P(),
            P("slab", None, None),
            P("slab", None, None),
            P("energy", "slab", None, None),
        ),
        out_specs=(P("energy", "slab", None, None), P(None, "slab", "energy", None)),
        check_vma=False,
    )
```
